256 devices in a mesh: queue: 32 (over x_hi, z, core), tensor: 8 (over y, x_lo).
Axes of the slice: x: 4 (x_hi: 2, x_lo: 2; x = x_hi * 2 + x_lo), y: 4, z: 8, core: 2. Of those that a mesh axis runs over, the one named last changes fastest.
Arguments:
- latents: bfloat16 [8192, 5120], P('queue', 'tensor')
- fresh_noise: bfloat16 [256, 5120], P(None, 'tensor')
- frame_level: int32 [32], P('queue'), may hold values from 0 to 63, as said below
- timestep_table: int32 [65], replicated, may hold values from 0 to 1000, as said below
- modulation: bfloat16 [65, 3, 5120], P(None, None, 'tensor')
- w_query: bfloat16 [5120, 3072], P(None, 'tensor')
- w_key: bfloat16 [5120, 3072], P(None, 'tensor')
- w_value: bfloat16 [5120, 3072], P(None, 'tensor'), may hold values from -0.078125 to 0.078125
- qk_gain: float32 [2, 3072], P(None, 'tensor'), as said below
- w_out: bfloat16 [3072, 5120], P('tensor', 'queue'), may hold values from -0.109375 to 0.109375
- reach: int32 [8192], P('queue'), may hold values from 1 to 256
Outputs:
- latents_out: bfloat16 [8192, 5120], P('queue', 'tensor')
- velocity: bfloat16 [8192, 5120], P('queue', 'tensor')
The draws below stay inside these ranges and needn't reach their ends.
Inputs may be any that keep to these rules, and one draw needn't show every extreme that they name: frame_level[q] is 2 q or 2 q + 1; the first is 0 and the last is 63. `timestep_table`: strictly falling from 1000 at entry 0 to 0 at the last entry. `qk_gain`: positive.
All inputs are finite; a program needn't handle non-finite values.
Results may differ from the reference program's by a relative error of at most 0.02.
Values may be sent and summed in bfloat16 or wider, within the bound.
No kernel may reach another device: no remote copies, remote signals or barrier semaphores. Data moves between devices by JAX's collectives and lax.ppermute only.
A program may use at most 64 MiB of HBM per device.

```python
import jax
import jax.numpy as jnp
from jax import lax

D = 5120
HEADS = 24
HD = 128
ROWS = 256
TOKENS = 8192
LEVELS = 65
N_QUEUE = 32
N_TENSOR = 8


def shared_query(key):
    return jax.random.normal(key, (D, HEADS * HD), jnp.float32) * D ** (-0.5)


def queue_levels(key):
    picked = jax.random.fold_in(key, 1)
    extra = jax.random.randint(picked, (N_QUEUE,), 0, 2, jnp.int32)
    level = 2 * jnp.arange(N_QUEUE, dtype=jnp.int32) + extra
    return level.at[0].set(0).at[N_QUEUE - 1].set(2 * N_QUEUE - 1)


def feature_scaled(key, count, low, high):
    noise = jnp.clip(jax.random.normal(key, (count, D), jnp.float32), -6.0, 6.0)
    ramp = jnp.exp(jnp.linspace(jnp.log(low), jnp.log(high), D, dtype=jnp.float32))
    return noise * ramp[None, :]


def draw_latents(key, part):
    key = jax.random.fold_in(key, 7)
    return feature_scaled(key, TOKENS, 0.6, 1.6).astype(jnp.bfloat16)


def draw_fresh_noise(key, part):
    key = jax.random.fold_in(key, 8)
    return feature_scaled(key, ROWS, 0.6, 1.6).astype(jnp.bfloat16)


def draw_modulation(key, part):
    key = jax.random.fold_in(key, 9)
    key_shift, key_scale, key_gate, key_polarity = jax.random.split(key, 4)
    shape = (LEVELS, 1, D)
    shift = jnp.clip(jax.random.normal(key_shift, shape, jnp.float32), -3.0, 3.0)
    scale = jax.random.uniform(key_scale, shape, jnp.float32, -0.4, 0.6)
    magnitude = jax.random.uniform(key_gate, shape, jnp.float32, 2.0, 4.0)
    polarity = jnp.where(jax.random.bernoulli(key_polarity, 0.5, shape), 1.0, -1.0).astype(jnp.float32)
    gate = polarity * magnitude
    return jnp.concatenate([shift, scale, gate], axis=1).astype(jnp.bfloat16)


def draw_w_query(key, part):
    return shared_query(key).astype(jnp.bfloat16)


def draw_w_key(key, part):
    key = jax.random.fold_in(key, 5)
    own = jax.random.normal(key, (D, HEADS * HD), jnp.float32) * D ** (-0.5)
    return own.astype(jnp.bfloat16)


def draw_qk_gain(key, part):
    key = jax.random.fold_in(key, 6)
    first = jax.random.fold_in(key, 0)
    return jax.random.uniform(first, (2, HEADS * HD), jnp.float32, 0.9, 1.6)


def draw_frame_level(key, part):
    return queue_levels(key)


def draw_timestep_table(key, part):
    level = queue_levels(key)
    key = jax.random.fold_in(key, 2)
    count = LEVELS - 1
    used = jnp.zeros((count,), jnp.int32).at[level].set(1)
    powers = jax.random.randint(key, (count,), 0, 3, jnp.int32)
    weights = used * jnp.left_shift(jnp.ones((count,), jnp.int32), powers)
    running = jnp.cumsum(weights).astype(jnp.int32)
    total = running[count - 1]
    spare = 1000 - count
    index = jnp.arange(1, LEVELS, dtype=jnp.int32)
    falls = index + spare * running // total
    table = 1000 - jnp.concatenate([jnp.zeros((1,), jnp.int32), falls.astype(jnp.int32)])
    return table.astype(jnp.int32)


def draw_reach(key, part):
    key = jax.random.fold_in(key, 3)
    first, second, third = jax.random.split(key, 3)
    values = jax.random.randint(first, (TOKENS,), 1, ROWS + 1, jnp.int32)
    high = jax.random.randint(second, (), 0, TOKENS, jnp.int32)
    low = (high + 1 + jax.random.randint(third, (), 0, TOKENS - 1, jnp.int32)) % TOKENS
    return values.at[high].set(ROWS).at[low].set(1)


def block_scale(key, extent, pieces, least, top_value):
    level = 1.0
    for axis_at, shards_of in pieces:
        steps = jax.random.uniform(jax.random.fold_in(jax.random.fold_in(key, 6), axis_at), (shards_of,), jnp.float32, least / len(pieces), top_value / len(pieces))
        level = level * jnp.repeat(jnp.exp(steps), extent[axis_at] // shards_of).reshape((-1,) + (1,) * (len(extent) - 1 - axis_at))
    return level


def gaussian(own_key, extent, scale, most, cuts=(), held_as=jnp.bfloat16):
    array = scale * jax.random.normal(own_key, extent, jnp.float32)
    if cuts:
        array = array * block_scale(own_key, extent, cuts, -0.22, 0.18)
    return jnp.clip(array, -most, most).astype(held_as)


def setup_inputs(seed: int = 0) -> dict:
    key_of = jax.random.split(jax.random.key(seed), 12)
    return {
        "latents": draw_latents(jax.random.fold_in(key_of[11], 71), 0),
        "fresh_noise": draw_fresh_noise(jax.random.fold_in(key_of[11], 71), 0),
        "frame_level": draw_frame_level(jax.random.fold_in(key_of[11], 71), 0),
        "timestep_table": draw_timestep_table(jax.random.fold_in(key_of[11], 71), 0),
        "modulation": draw_modulation(jax.random.fold_in(key_of[11], 71), 0),
        "w_query": draw_w_query(jax.random.fold_in(key_of[11], 71), 0),
        "w_key": draw_w_key(jax.random.fold_in(key_of[11], 71), 0),
        "w_value": gaussian(key_of[7], (D, HEADS * HD), D ** -0.5, 0.078125, ((1, 8),)),
        "qk_gain": draw_qk_gain(jax.random.fold_in(key_of[11], 71), 0),
        "w_out": gaussian(key_of[9], (HEADS * HD, D), (HEADS * HD) ** -0.5, 0.109375, ((0, 8), (1, 32))),
        "reach": draw_reach(jax.random.fold_in(key_of[11], 71), 0),
    }


def head_norm(proj, gain):
    shaped = proj.reshape(proj.shape[0], HEADS, HD)
    scaled = shaped * lax.rsqrt(lax.optimization_barrier(jnp.mean(shaped * shaped, axis=-1, keepdims=True)) + 1e-06)
    return (scaled * gain.reshape(HEADS, HD)).reshape(proj.shape[0], HEADS * HD).astype(jnp.bfloat16)

def sublayer(frames, mod_rows, w_query, w_key, w_value, qk_gain, w_out, reach_rows):
    width = HEADS * HD
    xf = frames.astype(jnp.float32)
    mean = lax.optimization_barrier(jnp.mean(xf, axis=-1, keepdims=True))
    var = lax.optimization_barrier(jnp.mean(xf * xf, axis=-1, keepdims=True)) - mean * mean
    shift = mod_rows[:, 0:1, :]
    scale = mod_rows[:, 1:2, :]
    gate = mod_rows[:, 2:3, :]
    normed = ((xf - mean) * lax.rsqrt(var + 1e-06) * (1.0 + scale) + shift).astype(jnp.bfloat16)
    flat = normed.reshape(N_QUEUE * ROWS, D)
    query = head_norm(jnp.dot(flat, w_query, preferred_element_type=jnp.float32), qk_gain[0])
    key = head_norm(jnp.dot(flat, w_key, preferred_element_type=jnp.float32), qk_gain[1])
    value = jnp.dot(flat, w_value, preferred_element_type=jnp.float32).astype(jnp.bfloat16)
    query = query.reshape(N_QUEUE, ROWS, width)
    zero_frame = jnp.zeros((1, ROWS, width), jnp.bfloat16)
    key_pad = jnp.concatenate([zero_frame, key.reshape(N_QUEUE, ROWS, width), zero_frame], axis=0)
    value_pad = jnp.concatenate([zero_frame, value.reshape(N_QUEUE, ROWS, width), zero_frame], axis=0)
    block_of = jnp.arange(3 * ROWS, dtype=jnp.int32) // ROWS
    spatial_key = jnp.arange(3 * ROWS, dtype=jnp.int32) % ROWS
    spatial_query = jnp.arange(ROWS, dtype=jnp.int32)

    def one_frame(frame):
        frame = frame.astype(jnp.int32)
        keys = lax.dynamic_slice_in_dim(key_pad, frame, 3, 0).reshape(3 * ROWS, HEADS, HD)
        values = lax.dynamic_slice_in_dim(value_pad, frame, 3, 0).reshape(3 * ROWS, HEADS, HD)
        queries = lax.dynamic_index_in_dim(query, frame, 0, keepdims=False).reshape(ROWS, HEADS, HD)
        reach_here = lax.dynamic_index_in_dim(reach_rows, frame, 0, keepdims=False)
        scores = jnp.einsum('rhd,khd->hrk', queries.astype(jnp.float32), keys.astype(jnp.float32)) * HD ** (-0.5)
        near = jnp.abs(spatial_key[None, :] - spatial_query[:, None]) < reach_here[:, None]
        exists = (block_of == 0) & (frame > 0) | (block_of == 2) & (frame < N_QUEUE - 1)
        visible = (block_of[None, :] == 1) | near & exists[None, :]
        scores = jnp.where(visible[None], scores, -1e+30)
        top = lax.optimization_barrier(jnp.max(scores, axis=-1, keepdims=True))
        weights = jnp.exp(scores - top)
        probs = (weights / lax.optimization_barrier(jnp.sum(weights, axis=-1, keepdims=True))).astype(jnp.bfloat16)
        attended = jnp.einsum('hrk,khd->rhd', probs.astype(jnp.float32), values.astype(jnp.float32))
        return attended.astype(jnp.bfloat16).reshape(ROWS, width)
    attended = lax.map(one_frame, jnp.arange(N_QUEUE, dtype=jnp.int32)).reshape(N_QUEUE * ROWS, width)
    group = width // N_TENSOR
    projected = jnp.zeros((N_QUEUE * ROWS, D), jnp.float32)
    for index in range(N_TENSOR):
        part_sum = jnp.dot(attended[:, index * group:(index + 1) * group], w_out[index * group:(index + 1) * group], preferred_element_type=jnp.float32)
        rounded = lax.optimization_barrier(part_sum.astype(jnp.bfloat16))
        projected = projected + rounded.astype(jnp.float32)
    return xf + gate * projected.reshape(N_QUEUE, ROWS, D)

def reference(latents, fresh_noise, frame_level, timestep_table, modulation, w_query, w_key, w_value, qk_gain, w_out, reach):
    mod_rows = modulation[frame_level].astype(jnp.float32)
    t_now = timestep_table[frame_level]
    t_next = timestep_table[frame_level + 1]
    step_size = ((t_next - t_now).astype(jnp.float32) / 1000.0)[:, None, None]
    reach_rows = reach.reshape(N_QUEUE, ROWS)
    frames = latents.reshape(N_QUEUE, ROWS, D)
    first = sublayer(frames, mod_rows, w_query, w_key, w_value, qk_gain, w_out, reach_rows)
    updated = (frames.astype(jnp.float32) + step_size * first).astype(jnp.bfloat16)
    advanced = jnp.concatenate([fresh_noise[None], updated[:-1]], axis=0)
    second = sublayer(advanced, mod_rows, w_query, w_key, w_value, qk_gain, w_out, reach_rows)
    latents_out = (advanced.astype(jnp.float32) + step_size * second).astype(jnp.bfloat16)
    velocity = second.astype(jnp.bfloat16)
    return (latents_out.reshape(TOKENS, D), velocity.reshape(TOKENS, D))
```

```python
import jax
import jax.numpy as jnp
from jax import lax
from jax.sharding import PartitionSpec as P

D = 5120
HD = 128
ROWS = 256
NQ = 32
NT = 8
MODROWS = 16
BOTH = ("queue", "tensor")


def t_of(y, x):
    return (y % 4) * 2 + x % 2


def q_of(h, z, c):
    return ((h % 2) * 8 + z % 8) * 2 + c % 2


def along_tensor(move):
    return [(t_of(y, x), move(y, x)) for y in range(4) for x in range(2)]


def along_queue(move):
    return [(q_of(h, z, c), move(h, z, c)) for h in range(2) for z in range(8) for c in range(2)]


SIDE = along_tensor(lambda y, x: t_of(y, x + 1))
UP = along_tensor(lambda y, x: t_of(y + 1, x))
DOWN = along_tensor(lambda y, x: t_of(y - 1, x))
FAR = along_queue(lambda h, z, c: q_of(h + 1, z, c))
NEXT = along_queue(lambda h, z, c: q_of(h, z + 1, c))
PREV = along_queue(lambda h, z, c: q_of(h, z - 1, c))
CORE = along_queue(lambda h, z, c: q_of(h, z, c + 1))


def next_frame(move):
    return [
        (q * NT + t_of(y, x), ((q + 1) % NQ) * NT + move(y, x))
        for q in range(NQ)
        for y in range(4)
        for x in range(2)
    ]


def spread(first, cut):
    own, side, below, above = first
    far_top = lax.ppermute(below[:cut], "tensor", UP)
    far_low = lax.ppermute(above[cut:], "tensor", DOWN)
    side_below = lax.ppermute(side, "tensor", UP)
    side_above = lax.ppermute(side, "tensor", DOWN)
    far = jnp.concatenate([far_top, far_low], axis=0)
    side_far = lax.ppermute(far, "tensor", SIDE)
    return [own, side, below, above, far, side_below, side_above, side_far]


def gather_blocks(block, cut):
    side = lax.ppermute(block, "tensor", SIDE)
    below = lax.ppermute(block, "tensor", UP)
    above = lax.ppermute(block, "tensor", DOWN)
    return spread((block, side, below, above), cut)


def gather_next(block, cut):
    own = lax.ppermute(block, BOTH, next_frame(lambda y, x: t_of(y, x)))
    side = lax.ppermute(block, BOTH, next_frame(lambda y, x: t_of(y, x + 1)))
    below = lax.ppermute(block, BOTH, next_frame(lambda y, x: t_of(y + 1, x)))
    above = lax.ppermute(block, BOTH, next_frame(lambda y, x: t_of(y - 1, x)))
    return spread((own, side, below, above), cut)


def source_ids():
    t = lax.axis_index("tensor")
    y, x = t // 2, t % 2

    def tid(dy, dx):
        return ((y + dy) % 4) * 2 + (x + dx) % 2

    return [tid(0, 0), tid(0, 1), tid(-1, 0), tid(1, 0), tid(2, 0), tid(-1, 1), tid(1, 1), tid(2, 1)]


def in_order(blocks, ids):
    width = blocks[0].shape[1]
    whole = jnp.zeros((blocks[0].shape[0], NT * width), blocks[0].dtype)
    for block, at in zip(blocks, ids):
        whole = lax.dynamic_update_slice(whole, block, (0, at * width))
    return whole


def gather_w_out(w_out):
    q = lax.axis_index("queue")
    h, z, c = q // 16, (q // 2) % 8, q % 2
    j = q % 4
    pieces = []
    for s in range(4):
        sub = lax.dynamic_slice_in_dim(w_out, ((j + s) % 4) * 96, 96, 0)
        route = []
        for t in range(NT):
            for jj in range(4):
                for a in range(NT):
                    r = 4 * a + (jj + s) % 4
                    rc, rz, rh = r // 16, (r // 2) % 8, r % 2
                    route.append(((4 * t + jj) * NT + a, q_of(rh, rz, rc) * NT + t))
        pieces.append(lax.ppermute(sub, BOTH, route))
    row = (c * 8 + z) * 2 + h
    stacked = jnp.stack(pieces)
    chunk = jnp.concatenate(
        [lax.dynamic_index_in_dim(stacked, (row - jj) % 4, 0, keepdims=False) for jj in range(4)],
        axis=1,
    )
    other = lax.ppermute(chunk, "queue", FAR)
    pair = jnp.where(h == 0, jnp.stack([chunk, other]), jnp.stack([other, chunk]))
    half = jnp.zeros((8,) + pair.shape, pair.dtype)
    half = lax.dynamic_update_slice(half, pair[None], (z, 0, 0, 0))
    up = down = pair
    for k in range(1, 5):
        up = lax.ppermute(up, "queue", NEXT)
        half = lax.dynamic_update_slice(half, up[None], ((z - k) % 8, 0, 0, 0))
        if k < 4:
            down = lax.ppermute(down, "queue", PREV)
            half = lax.dynamic_update_slice(half, down[None], ((z + k) % 8, 0, 0, 0))
    swapped = lax.ppermute(half, "queue", CORE)
    whole = jnp.where(c == 0, jnp.stack([half, swapped]), jnp.stack([swapped, half]))
    return whole.reshape(3072, 640)


def head_norm(proj, gain, heads_here):
    shaped = proj.reshape(proj.shape[0], heads_here, HD)
    scaled = shaped * lax.rsqrt(jnp.mean(shaped * shaped, axis=-1, keepdims=True) + 1e-06)
    return (
        (scaled * gain.reshape(heads_here, HD))
        .reshape(proj.shape[0], heads_here * HD)
        .astype(jnp.bfloat16)
    )


def body(
    latents,
    fresh_noise,
    frame_level,
    timestep_table,
    modulation,
    w_query,
    w_key,
    w_value,
    qk_gain,
    w_out,
    reach,
):
    rows = latents.shape[0]
    width_here = w_query.shape[1]
    heads_here = width_here // HD
    position = lax.axis_index("queue")
    level = frame_level[0]
    mod_rows = lax.dynamic_index_in_dim(modulation, level, 0, keepdims=False)
    gate = mod_rows[2].astype(jnp.float32)
    t_now = lax.dynamic_index_in_dim(timestep_table, level, 0, keepdims=False)
    t_next = lax.dynamic_index_in_dim(timestep_table, level + 1, 0, keepdims=False)
    step_size = (t_next - t_now).astype(jnp.float32) / 1000.0
    block_of = jnp.arange(3 * rows, dtype=jnp.int32) // rows
    spatial_key = jnp.arange(3 * rows, dtype=jnp.int32) % rows
    spatial_query = jnp.arange(rows, dtype=jnp.int32)
    near = jnp.abs(spatial_key[None, :] - spatial_query[:, None]) < reach[:, None]
    exists = (block_of == 0) & (position > 0) | (block_of == 2) & (position < NQ - 1)
    visible = (block_of[None, :] == 1) | near & exists[None, :]
    ids = source_ids()
    to_next = [(i, i + 1) for i in range(NQ - 1)]
    to_prev = [(i + 1, i) for i in range(NQ - 1)]

    def attend(frame, shift, scale):
        xf = frame.astype(jnp.float32)
        mean = jnp.mean(xf, axis=1, keepdims=True)
        var = jnp.mean(xf * xf, axis=1, keepdims=True) - mean * mean
        normed = ((xf - mean) * lax.rsqrt(var + 1e-06) * (1.0 + scale) + shift).astype(jnp.bfloat16)
        key = head_norm(
            jnp.dot(normed, w_key, preferred_element_type=jnp.float32), qk_gain[1], heads_here
        )
        value = jnp.dot(normed, w_value, preferred_element_type=jnp.float32).astype(jnp.bfloat16)
        both = jnp.stack([key, value], axis=0)
        low = lax.ppermute(both, "queue", to_next)
        high = lax.ppermute(both, "queue", to_prev)
        query = head_norm(
            jnp.dot(normed, w_query, preferred_element_type=jnp.float32), qk_gain[0], heads_here
        )
        widened = jnp.concatenate([low, both, high], axis=1)
        keys = widened[0].reshape(3 * rows, heads_here, HD)
        values = widened[1].reshape(3 * rows, heads_here, HD)
        queries = query.reshape(rows, heads_here, HD)
        scores = jnp.einsum(
            "rhd,khd->hrk", queries, keys, preferred_element_type=jnp.float32
        ) * HD ** (-0.5)
        scores = jnp.where(visible[None], scores, -1e30)
        top = jnp.max(scores, axis=-1, keepdims=True)
        weights = jnp.exp(scores - top)
        probs = (weights / jnp.sum(weights, axis=-1, keepdims=True)).astype(jnp.bfloat16)
        attended = jnp.einsum("hrk,khd->rhd", probs, values, preferred_element_type=jnp.float32)
        return attended.astype(jnp.bfloat16).reshape(rows, width_here)

    def project(attended, w_whole):
        whole = in_order(gather_blocks(attended, 128), ids)
        return jnp.dot(whole, w_whole, preferred_element_type=jnp.float32)

    payload = jnp.concatenate(
        [latents, mod_rows[:2], jnp.zeros((MODROWS - 2, latents.shape[1]), latents.dtype)], axis=0
    )
    gathered = in_order(gather_blocks(payload, 144), ids)
    shift = gathered[rows : rows + 1].astype(jnp.float32)
    scale = gathered[rows + 1 : rows + 2].astype(jnp.float32)
    w_whole = gather_w_out(w_out)

    attended = attend(gathered[:rows], shift, scale)
    xf = latents.astype(jnp.float32)
    first = xf + gate * project(attended, w_whole)
    updated = (xf + step_size * first).astype(jnp.bfloat16)

    leaving = jnp.where(position == NQ - 1, fresh_noise, updated)
    blocks = gather_next(leaving, 128)
    attended = attend(in_order(blocks, ids), shift, scale)
    xf = blocks[0].astype(jnp.float32)
    second = xf + gate * project(attended, w_whole)
    latents_out = (xf + step_size * second).astype(jnp.bfloat16)
    return (latents_out, second.astype(jnp.bfloat16))


def solution(mesh):
    placed = (
        P("queue", "tensor"),
        P(None, "tensor"),
        P("queue"),
        P(),
        P(None, None, "tensor"),
        P(None, "tensor"),
        P(None, "tensor"),
        P(None, "tensor"),
        P(None, "tensor"),
        P("tensor", "queue"),
        P("queue"),
    )
    return jax.shard_map(
        body,
        mesh=mesh,
        in_specs=placed,
        out_specs=(P("queue", "tensor"), P("queue", "tensor")),
        check_vma=False,
    )
```

```python
import jax
import jax.numpy as jnp
from jax import lax
from jax.experimental import pallas as pl
from jax.experimental.pallas import tpu as pltpu
from jax.sharding import PartitionSpec as P

D = 5120
HD = 128
ROWS = 256
NQ = 32
NT = 8
MODROWS = 16
BOTH = ("queue", "tensor")


def t_of(y, x):
    return (y % 4) * 2 + x % 2


def q_of(h, z, c):
    return ((h % 2) * 8 + z % 8) * 2 + c % 2


def along_tensor(move):
    return [(t_of(y, x), move(y, x)) for y in range(4) for x in range(2)]


def along_queue(move):
    return [(q_of(h, z, c), move(h, z, c)) for h in range(2) for z in range(8) for c in range(2)]


SIDE = along_tensor(lambda y, x: t_of(y, x + 1))
UP = along_tensor(lambda y, x: t_of(y + 1, x))
DOWN = along_tensor(lambda y, x: t_of(y - 1, x))
FAR = along_queue(lambda h, z, c: q_of(h + 1, z, c))
NEXT = along_queue(lambda h, z, c: q_of(h, z + 1, c))
PREV = along_queue(lambda h, z, c: q_of(h, z - 1, c))
CORE = along_queue(lambda h, z, c: q_of(h, z, c + 1))


def next_frame(move):
    return [
        (q * NT + t_of(y, x), ((q + 1) % NQ) * NT + move(y, x))
        for q in range(NQ)
        for y in range(4)
        for x in range(2)
    ]


def spread(first, cut):
    own, side, below, above = first
    far_top = lax.ppermute(below[:cut], "tensor", UP)
    far_low = lax.ppermute(above[cut:], "tensor", DOWN)
    side_below = lax.ppermute(side, "tensor", UP)
    side_above = lax.ppermute(side, "tensor", DOWN)
    far = jnp.concatenate([far_top, far_low], axis=0)
    side_far = lax.ppermute(far, "tensor", SIDE)
    return [own, side, below, above, far, side_below, side_above, side_far]


def gather_blocks(block, cut):
    side = lax.ppermute(block, "tensor", SIDE)
    below = lax.ppermute(block, "tensor", UP)
    above = lax.ppermute(block, "tensor", DOWN)
    return spread((block, side, below, above), cut)


def gather_next(block, cut):
    own = lax.ppermute(block, BOTH, next_frame(lambda y, x: t_of(y, x)))
    side = lax.ppermute(block, BOTH, next_frame(lambda y, x: t_of(y, x + 1)))
    below = lax.ppermute(block, BOTH, next_frame(lambda y, x: t_of(y + 1, x)))
    above = lax.ppermute(block, BOTH, next_frame(lambda y, x: t_of(y - 1, x)))
    return spread((own, side, below, above), cut)


def source_ids():
    t = lax.axis_index("tensor")
    y, x = t // 2, t % 2

    def tid(dy, dx):
        return ((y + dy) % 4) * 2 + (x + dx) % 2

    return [tid(0, 0), tid(0, 1), tid(-1, 0), tid(1, 0), tid(2, 0), tid(-1, 1), tid(1, 1), tid(2, 1)]


def gather_w_out(w_out, after):
    q = lax.axis_index("queue")
    h = q // 16
    turned, _ = lax.optimization_barrier((w_out.T, after))

    def deliver(flip):
        route = []
        for t in range(NT):
            for j in range(4):
                for a in range(NT):
                    route.append(((4 * t + j) * NT + a, q_of(j % 2 + flip, a, j // 2) * NT + t))
        return lax.ppermute(turned, BOTH, route)

    straight, crossed = deliver(0), deliver(1)
    pair = jnp.where(
        h == 0,
        jnp.concatenate([straight, crossed], axis=0),
        jnp.concatenate([crossed, straight], axis=0),
    )
    ups, downs = [pair], []
    down = pair
    for k in range(1, 5):
        ups.append(lax.ppermute(ups[-1], "queue", NEXT))
        if k < 4:
            down = lax.ppermute(down, "queue", PREV)
            downs.append(down)
    half = jnp.stack(ups + downs[::-1])
    swapped = lax.ppermute(half, "queue", CORE)
    return half, swapped


def nt_dot(a, b):
    return lax.dot_general(a, b, (((1,), (1,)), ((), ())), preferred_element_type=jnp.float32)


def head_norm(proj, gain):
    scale = lax.rsqrt(jnp.mean(proj * proj, axis=-1, keepdims=True) + 1e-06)
    return (proj * scale * gain).astype(jnp.bfloat16)


def normalise(ids_ref, blocks, mods_ref, normed_ref):
    chunk = 32

    def rows_at(r, carry):
        at = pl.ds(pl.multiple_of(r * chunk, chunk), chunk)
        total = jnp.zeros((chunk, HD), jnp.float32)
        squares = jnp.zeros((chunk, HD), jnp.float32)
        for block in blocks:
            for j in range(5):
                x = block[at, j * HD : (j + 1) * HD].astype(jnp.float32)
                total = total + x
                squares = squares + x * x
        mean = jnp.sum(total, axis=1, keepdims=True) / D
        var = jnp.sum(squares, axis=1, keepdims=True) / D - mean * mean
        inverse = lax.rsqrt(var + 1e-06)
        for i, block in enumerate(blocks):
            base = ids_ref[i] * 640
            for j in range(5):
                cols = pl.ds(pl.multiple_of(base + j * HD, HD), HD)
                x = block[at, j * HD : (j + 1) * HD].astype(jnp.float32)
                shift = mods_ref[0:1, cols].astype(jnp.float32)
                scale = mods_ref[1:2, cols].astype(jnp.float32)
                y = (x - mean) * inverse * (1.0 + scale) + shift
                normed_ref[at, cols] = y.astype(jnp.bfloat16)
        return carry

    lax.fori_loop(0, ROWS // chunk, rows_at, 0)


def key_value_first(ids_ref, *refs):
    blocks = refs[:8]
    gain_ref, wk_ref, wv_ref, mods_ref, normed_ref, kv_ref = refs[8:]

    @pl.when(pl.program_id(0) == 0)
    def _():
        for i, block in enumerate(blocks):
            cols = pl.ds(pl.multiple_of(ids_ref[i] * 640, HD), 640)
            mods_ref[:, cols] = block[ROWS : ROWS + MODROWS, :]

    key_value(ids_ref, blocks, mods_ref, gain_ref, wk_ref, wv_ref, normed_ref, kv_ref)


def key_value_later(ids_ref, *refs):
    blocks = refs[:8]
    mods_ref, gain_ref, wk_ref, wv_ref, normed_ref, kv_ref = refs[8:]
    key_value(ids_ref, blocks, mods_ref, gain_ref, wk_ref, wv_ref, normed_ref, kv_ref)


def key_value(ids_ref, blocks, mods_ref, gain_ref, wk_ref, wv_ref, normed_ref, kv_ref):
    step = pl.program_id(0)

    @pl.when(step == 0)
    def _():
        normalise(ids_ref, blocks, mods_ref, normed_ref)

    @pl.when(step < 3)
    def _():
        proj = jnp.dot(normed_ref[...], wk_ref[...], preferred_element_type=jnp.float32)
        kv_ref[0] = head_norm(proj, gain_ref[0])

    @pl.when(step >= 3)
    def _():
        proj = jnp.dot(normed_ref[...], wv_ref[...], preferred_element_type=jnp.float32)
        kv_ref[0] = proj.astype(jnp.bfloat16)


def whole(shape):
    return pl.BlockSpec(shape, lambda i: (0,) * len(shape))


def run_key_value(ids, blocks, mods, gain, w_key, w_value):
    rows = blocks[0].shape[0]
    first = mods is None
    out_shape = [
        jax.ShapeDtypeStruct((ROWS, D), jnp.bfloat16),
        jax.ShapeDtypeStruct((6, ROWS, HD), jnp.bfloat16),
    ]
    out_specs = [whole((ROWS, D)), pl.BlockSpec((1, ROWS, HD), lambda i: (i, 0, 0))]
    in_specs = [pl.BlockSpec(memory_space=pltpu.SMEM)] + [whole((rows, 640))] * 8
    args = [ids, *blocks]
    if first:
        out_shape.insert(0, jax.ShapeDtypeStruct((MODROWS, D), jnp.bfloat16))
        out_specs.insert(0, whole((MODROWS, D)))
    else:
        in_specs.append(whole((MODROWS, D)))
        args.append(mods)
    in_specs += [
        pl.BlockSpec((1, 1, HD), lambda i: (3 + jnp.minimum(i, 2), 0, 0)),
        pl.BlockSpec((D, HD), lambda i: (0, jnp.minimum(i, 2))),
        pl.BlockSpec((D, HD), lambda i: (0, jnp.maximum(i - 3, 0))),
    ]
    out = pl.pallas_call(
        key_value_first if first else key_value_later,
        grid=(6,),
        in_specs=in_specs,
        out_specs=out_specs,
        out_shape=out_shape,
        compiler_params=pltpu.CompilerParams(vmem_limit_bytes=40 * 2**20),
        cost_estimate=pl.CostEstimate(
            flops=2 * ROWS * D * 768, bytes_accessed=D * 768 * 2 + 3 * ROWS * D * 2, transcendentals=0
        ),
        name="norm_key_value",
    )(*args, gain, w_key, w_value)
    return out if first else [mods, *out]


LOG2E = 1.4426950408889634
SCORE = HD ** (-0.5) * LOG2E


def query_own(normed_ref, wq_ref, gain_ref, k_ref, v_ref, q_ref, top_ref, sum_ref, acc_ref):
    proj = jnp.dot(normed_ref[...], wq_ref[...], preferred_element_type=jnp.float32)
    q = head_norm(proj, gain_ref[0])
    q_ref[0] = q
    scores = nt_dot(q, k_ref[0]) * SCORE
    top = jnp.max(scores, axis=-1, keepdims=True)
    weights = jnp.exp2(scores - top)
    top_ref[0] = jnp.broadcast_to(top, (ROWS, HD))
    sum_ref[0] = jnp.broadcast_to(jnp.sum(weights, axis=-1, keepdims=True), (ROWS, HD))
    acc_ref[0] = jnp.dot(
        weights.astype(jnp.bfloat16), v_ref[0], preferred_element_type=jnp.float32
    )


def head_spec(offset=0):
    return pl.BlockSpec((1, ROWS, HD), lambda i: (i + offset, 0, 0))


def run_query_own(normed, w_query, gain, kv):
    wide = jax.ShapeDtypeStruct((3, ROWS, HD), jnp.float32)
    return pl.pallas_call(
        query_own,
        grid=(3,),
        in_specs=[
            whole((ROWS, D)),
            pl.BlockSpec((D, HD), lambda i: (0, i)),
            pl.BlockSpec((1, 1, HD), lambda i: (i, 0, 0)),
            head_spec(),
            head_spec(3),
        ],
        out_specs=[head_spec()] * 4,
        out_shape=[jax.ShapeDtypeStruct((3, ROWS, HD), jnp.bfloat16), wide, wide, wide],
        compiler_params=pltpu.CompilerParams(vmem_limit_bytes=32 * 2**20),
        cost_estimate=pl.CostEstimate(
            flops=2 * ROWS * (D + 512) * 384, bytes_accessed=D * 384 * 2 + ROWS * D * 2, transcendentals=3 * ROWS * ROWS
        ),
        name="query_own",
    )(normed, w_query, gain, kv, kv)


def neighbours(
    at_ref, reach_ref, q_ref, top_ref, sum_ref, acc_ref, kl_ref, vl_ref, kh_ref, vh_ref, out_ref
):
    position = at_ref[8]
    q = q_ref[0]
    row = lax.broadcasted_iota(jnp.int32, (ROWS, ROWS), 0)
    col = lax.broadcasted_iota(jnp.int32, (ROWS, ROWS), 1)
    reach = reach_ref[...]
    near = jnp.abs(col - row) < reach
    low_reach = jnp.where(position > 0, reach, 0)
    high_reach = jnp.where(position < NQ - 1, reach, 0)
    low_near = jnp.abs(col - row) < low_reach
    high_near = jnp.abs(col - row) < high_reach
    low = jnp.where(low_near, nt_dot(q, kl_ref[0]) * SCORE, -1e30)
    high = jnp.where(high_near, nt_dot(q, kh_ref[0]) * SCORE, -1e30)
    own_top = top_ref[0][:, :1]
    top = jnp.maximum(own_top, jnp.max(jnp.maximum(low, high), axis=-1, keepdims=True))
    own_scale = jnp.exp2(own_top - top)
    low = jnp.exp2(low - top)
    high = jnp.exp2(high - top)
    total = sum_ref[0][:, :1] * own_scale + jnp.sum(low + high, axis=-1, keepdims=True)
    acc = acc_ref[0] * own_scale
    acc = acc + jnp.dot(low.astype(jnp.bfloat16), vl_ref[0], preferred_element_type=jnp.float32)
    acc = acc + jnp.dot(high.astype(jnp.bfloat16), vh_ref[0], preferred_element_type=jnp.float32)
    out_ref[...] = (acc / total).astype(jnp.bfloat16)


def run_neighbours(ids, reach, q, top, total, acc, low, high):
    return pl.pallas_call(
        neighbours,
        grid=(3,),
        in_specs=[pl.BlockSpec(memory_space=pltpu.SMEM), whole((ROWS, 1))]
        + [head_spec()] * 4
        + [head_spec(), head_spec(3), head_spec(), head_spec(3)],
        out_specs=pl.BlockSpec((ROWS, HD), lambda i: (0, i)),
        out_shape=jax.ShapeDtypeStruct((ROWS, 3 * HD), jnp.bfloat16),
        compiler_params=pltpu.CompilerParams(vmem_limit_bytes=24 * 2**20),
        cost_estimate=pl.CostEstimate(
            flops=2 * ROWS * 1024 * 384, bytes_accessed=3 * 2**20, transcendentals=6 * ROWS * ROWS
        ),
        name="neighbours",
    )(ids, reach, q, top, total, acc, low, low, high, high)


def projected(ids_ref, step_ref, refs, w_ref):
    blocks = refs[:8]
    half_ref, swapped_ref, x_ref, gate_ref = refs[8:12]
    z, c = ids_ref[9], ids_ref[10]

    def place(i, carry):
        w_ref[i, pl.ds(pl.multiple_of(c * 320, 64), 320), :] = half_ref[i]
        w_ref[i, pl.ds(pl.multiple_of((1 - c) * 320, 64), 320), :] = swapped_ref[i]
        return carry

    lax.fori_loop(0, 8, place, 0)
    total = jnp.zeros((ROWS, 640), jnp.float32)
    for i, block in enumerate(blocks):
        total = total + nt_dot(block[...], w_ref[lax.rem(z - ids_ref[i] + 8, 8)])
    x = x_ref[...].astype(jnp.float32)
    result = x + gate_ref[...] * total
    after = (x + step_ref[0] * result).astype(jnp.bfloat16)
    return result, after


def project(ids_ref, step_ref, *refs):
    fresh_ref, out_ref, w_ref = refs[12:]
    _, after = projected(ids_ref, step_ref, refs, w_ref)
    out_ref[...] = jnp.where(ids_ref[8] == NQ - 1, fresh_ref[...], after)


def project_last(ids_ref, step_ref, *refs):
    out_ref, velocity_ref, w_ref = refs[12:]
    result, after = projected(ids_ref, step_ref, refs, w_ref)
    out_ref[...] = after
    velocity_ref[...] = result.astype(jnp.bfloat16)


def run_project(ids, step_size, blocks, halves, x, gate, fresh=None):
    block = jax.ShapeDtypeStruct((ROWS, 640), jnp.bfloat16)
    vmem = pl.BlockSpec(memory_space=pltpu.VMEM)
    smem = pl.BlockSpec(memory_space=pltpu.SMEM)
    more = [fresh] if fresh is not None else []
    return pl.pallas_call(
        project if fresh is not None else project_last,
        in_specs=[smem, smem] + [vmem] * (12 + len(more)),
        out_specs=vmem if more else [vmem, vmem],
        out_shape=block if more else [block, block],
        scratch_shapes=[pltpu.VMEM((8, 640, 384), jnp.bfloat16)],
        compiler_params=pltpu.CompilerParams(vmem_limit_bytes=32 * 2**20),
        cost_estimate=pl.CostEstimate(
            flops=2 * ROWS * 3072 * 640, bytes_accessed=8 * 2**20, transcendentals=0
        ),
        name="project",
    )(ids, step_size, *blocks, *halves, x, gate, *more)


def body(
    latents,
    fresh_noise,
    frame_level,
    timestep_table,
    modulation,
    w_query,
    w_key,
    w_value,
    qk_gain,
    w_out,
    reach,
):
    q = lax.axis_index("queue")
    level = frame_level[0]
    mod_rows = lax.dynamic_index_in_dim(modulation, level, 0, keepdims=False)
    gate = mod_rows[2:3].astype(jnp.float32)
    t_now = lax.dynamic_index_in_dim(timestep_table, level, 0, keepdims=False)
    t_next = lax.dynamic_index_in_dim(timestep_table, level + 1, 0, keepdims=False)
    step_size = ((t_next - t_now).astype(jnp.float32) / 1000.0)[None]
    ids = jnp.stack(source_ids() + [q, (q // 2) % 8, q % 2]).astype(jnp.int32)
    gain = qk_gain.reshape(6, 1, HD)
    reach_rows = reach[:, None]
    to_next = [(i, i + 1) for i in range(NQ - 1)]
    to_prev = [(i + 1, i) for i in range(NQ - 1)]

    def attend(blocks, mods):
        mods, normed, kv = run_key_value(ids, blocks, mods, gain, w_key, w_value)
        low = lax.ppermute(kv, "queue", to_next)
        high = lax.ppermute(kv, "queue", to_prev)
        own = run_query_own(normed, w_query, gain, kv)
        attended = run_neighbours(ids, reach_rows, *own, low, high)
        return mods, gather_blocks(attended, 128)

    payload = jnp.concatenate(
        [latents, mod_rows[:2], jnp.zeros((MODROWS - 2, latents.shape[1]), latents.dtype)], axis=0
    )
    blocks = gather_blocks(payload, 144)
    halves = gather_w_out(w_out, blocks[1])
    mods, attended = attend(blocks, None)
    leaving = run_project(ids, step_size, attended, halves, latents, gate, fresh_noise)

    blocks = gather_next(leaving, 128)
    mods, attended = attend(blocks, mods)
    return tuple(run_project(ids, step_size, attended, halves, blocks[0], gate))


def solution(mesh):
    placed = (
        P("queue", "tensor"),
        P(None, "tensor"),
        P("queue"),
        P(),
        P(None, None, "tensor"),
        P(None, "tensor"),
        P(None, "tensor"),
        P(None, "tensor"),
        P(None, "tensor"),
        P("tensor", "queue"),
        P("queue"),
    )
    return jax.shard_map(
        body,
        mesh=mesh,
        in_specs=placed,
        out_specs=(P("queue", "tensor"), P("queue", "tensor")),
        check_vma=False,
    )
```

```python
import functools

import jax
import jax.numpy as jnp
from jax import lax
from jax.experimental import pallas as pl
from jax.experimental.pallas import tpu as pltpu
from jax.sharding import PartitionSpec as P

D = 5120
HD = 128
ROWS = 256
NQ = 32
NT = 8
MODROWS = 16
BOTH = ("queue", "tensor")


def t_of(y, x):
    return (y % 4) * 2 + x % 2


def q_of(h, z, c):
    return ((h % 2) * 8 + z % 8) * 2 + c % 2


def along_tensor(move):
    return [(t_of(y, x), move(y, x)) for y in range(4) for x in range(2)]


def along_queue(move):
    return [(q_of(h, z, c), move(h, z, c)) for h in range(2) for z in range(8) for c in range(2)]


def other_near(y):
    return (y + 1) % 4 if y % 2 else (y - 1) % 4


SIDE = along_tensor(lambda y, x: t_of(y, x + 1))
NEAR = along_tensor(lambda y, x: t_of(y ^ 1, x))
BACK = along_tensor(lambda y, x: t_of(other_near(y), x))
FAR = along_queue(lambda h, z, c: q_of(h + 1, z, c))
RING = [[q_of(h, z, c) for z in range(8) for c in range(2)] for h in range(2)]


def gather_blocks(block, start, early, late, hold=True):
    near = lax.ppermute(block, "tensor", NEAR)
    back = lax.ppermute(block, "tensor", BACK)
    side = lax.ppermute(block, "tensor", SIDE)
    begun = start(block)
    if hold:
        back, near, side, begun = lax.optimization_barrier((back, near, side, begun))
    far = lax.ppermute(back, "tensor", NEAR)
    side_back = lax.ppermute(side, "tensor", BACK)
    side_near = lax.ppermute(side, "tensor", NEAR)
    begun = early([side, near, back], begun)
    if hold:
        far, begun = lax.optimization_barrier((far, begun))
    side_far = lax.ppermute(far, "tensor", SIDE)
    going = late([far, side_near, side_back], begun)
    return side_far, going


def after(value, *others):
    return lax.optimization_barrier((value, *others))[0]


def source_ids():
    t = lax.axis_index("tensor")
    y, x = t // 2, t % 2
    near, back, far = y ^ 1, (y + 2 * (y % 2) - 1) % 4, y ^ 2
    pairs = [(y, x), (y, 1 - x), (near, x), (back, x), (far, x), (near, 1 - x), (back, 1 - x), (far, 1 - x)]
    return [2 * a + b for a, b in pairs]


def transposed(block):
    route = [
        ((4 * t + j) * NT + a, (4 * a + j) * NT + t)
        for t in range(NT)
        for j in range(4)
        for a in range(NT)
    ]
    return lax.ppermute(block, BOTH, route)


def next_frame(block):
    return lax.ppermute(block, "queue", [(i, (i + 1) % NQ) for i in range(NQ)])


def nt_dot(a, b):
    return lax.dot_general(a, b, (((1,), (1,)), ((), ())), preferred_element_type=jnp.float32)


VMEM = pl.BlockSpec(memory_space=pltpu.VMEM)
SMEM = pl.BlockSpec(memory_space=pltpu.SMEM)
CHUNK = 64
TALL = ROWS + MODROWS


def add_stats(blocks, total_ref, square_ref, fresh):
    def rows_at(r, carry):
        at = pl.ds(pl.multiple_of(r * CHUNK, CHUNK), CHUNK)
        if fresh:
            total = jnp.zeros((CHUNK, HD), jnp.float32)
            square = jnp.zeros((CHUNK, HD), jnp.float32)
        else:
            total, square = total_ref[at, :], square_ref[at, :]
        for block in blocks:
            for j in range(5):
                x = block[at, j * HD : (j + 1) * HD].astype(jnp.float32)
                total = total + x
                square = square + x * x
        total_ref[at, :] = total
        square_ref[at, :] = square
        return carry

    lax.fori_loop(0, ROWS // CHUNK, rows_at, 0)


def scaled_block(block, mods, center_ref, a_ref):
    line = lax.broadcasted_iota(jnp.int32, (MODROWS, HD), 0)
    for j in range(5):
        cols = slice(j * HD, (j + 1) * HD)
        rows = mods[:, cols].astype(jnp.float32)
        shift, scale = rows[0:1], 1.0 + rows[1:2]
        high = scale.astype(jnp.bfloat16).astype(jnp.float32)
        extra = jnp.where(
            line == 0,
            shift,
            jnp.where(line == 1, high, jnp.where(line == 2, scale - high, 0.0)),
        )
        a_ref[ROWS:TALL, cols] = extra.astype(jnp.bfloat16)
        for r in range(0, ROWS, CHUNK):
            x = block[r : r + CHUNK, cols].astype(jnp.float32)
            y = (x - center_ref[r : r + CHUNK, :]) * scale
            a_ref[r : r + CHUNK, cols] = y.astype(jnp.bfloat16)


def add_products(which, a_ref, weights, out_ref, total_in):
    ids = source_ids()
    for n, w_ref in enumerate(weights):
        cols = slice(n * 384, (n + 1) * 384)
        total = None if total_in is None else total_in[:, cols]
        for i, at in enumerate(which):
            rows = pl.ds(pl.multiple_of(ids[at] * 640, HD), 640)
            part = jnp.dot(a_ref[i], w_ref[rows, :], preferred_element_type=jnp.float32)
            total = part if total is None else total + part
        out_ref[:, cols] = total


def scaled_blocks(blocks, mods_ref, given, center_ref, a_ref):
    for i, block in enumerate(blocks):
        if not given:
            mods_ref[i] = block[ROWS:TALL, :]
        scaled_block(block, mods_ref.at[i], center_ref, a_ref.at[i])


def split_refs(n, given, refs, scratches=1):
    blocks, refs = refs[:n], refs[n:]
    if given:
        return blocks, refs[0], refs[1:]
    at = len(refs) - scratches - 1
    return blocks, refs[at], refs[:at] + refs[at + 1 :]


def first_part(which, given, *refs):
    n = len(which)
    blocks, mods_ref, refs = split_refs(n, given, refs)
    wq, wk, wv, acc_ref, total_ref, square_ref, center_ref, a_ref = refs
    add_stats(blocks, total_ref, square_ref, True)
    center = jnp.sum(total_ref[...], axis=1, keepdims=True) / (n * 640)
    center_ref[...] = jnp.broadcast_to(center, (ROWS, HD))
    scaled_blocks(blocks, mods_ref, given, center_ref, a_ref)
    add_products(which, a_ref, (wq, wk, wv), acc_ref, None)


def middle_part(which, given, *refs):
    blocks, mods_ref, refs = split_refs(len(which), given, refs)
    wq, wk, wv, acc_in, total_in, square_in, center_ref = refs[:7]
    acc_ref, total_ref, square_ref, a_ref = refs[7:]
    total_ref[...] = total_in[...]
    square_ref[...] = square_in[...]
    add_stats(blocks, total_ref, square_ref, False)
    scaled_blocks(blocks, mods_ref, given, center_ref, a_ref)
    add_products(which, a_ref, (wq, wk, wv), acc_ref, acc_in)


def head_norm(proj, gain):
    scale = lax.rsqrt(jnp.mean(proj * proj, axis=-1, keepdims=True) + 1e-06)
    return (proj * scale * gain).astype(jnp.bfloat16)


def last_part(which, given, *refs):
    blocks, mods_ref, refs = split_refs(len(which), given, refs, 4)
    wq, wk, wv, acc_in, total_in, square_in, center_ref, gain_ref = refs[:8]
    q_ref, kv_ref = refs[8:10]
    acc_ref, total_ref, square_ref, a_ref = refs[10:]
    total_ref[...] = total_in[...]
    square_ref[...] = square_in[...]
    add_stats(blocks, total_ref, square_ref, False)
    scaled_blocks(blocks, mods_ref, given, center_ref, a_ref)
    add_products(which, a_ref, (wq, wk, wv), acc_ref, acc_in)
    mean = jnp.sum(total_ref[...], axis=1, keepdims=True) / D
    var = jnp.sum(square_ref[...], axis=1, keepdims=True) / D - mean * mean
    inverse = lax.rsqrt(var + 1e-06)
    offset = (center_ref[:, :1] - mean) * inverse
    for n in range(9):
        cols = slice(n * HD, (n + 1) * HD)
        extra = acc_ref[ROWS:TALL, cols]
        proj = acc_ref[:ROWS, cols] * inverse + offset * (extra[1:2] + extra[2:3]) + extra[0:1]
        if n < 3:
            q_ref[n] = head_norm(proj, gain_ref[n // 3 : n // 3 + 1, n % 3 * HD : (n % 3 + 1) * HD])
        elif n < 6:
            kv_ref[n - 3, 0] = head_norm(proj, gain_ref[n // 3 : n // 3 + 1, n % 3 * HD : (n % 3 + 1) * HD])
        else:
            kv_ref[n - 6, 1] = proj.astype(jnp.bfloat16)


def cost(flops, nbytes):
    return pl.CostEstimate(flops=flops, bytes_accessed=nbytes, transcendentals=0)


def run_part(kernel, which, blocks, mods, weights, state, gain=None):
    n = len(which)
    wide = jax.ShapeDtypeStruct((ROWS, HD), jnp.float32)
    acc = jax.ShapeDtypeStruct((TALL, 1152), jnp.float32)
    args = [*blocks] + ([] if mods is None else [mods])
    args += [*weights, *state] + ([] if gain is None else [gain])
    scratch = [
        pltpu.VMEM((n, TALL, 640), jnp.bfloat16),
    ]
    if gain is not None:
        out_shape = [
            jax.ShapeDtypeStruct((3, ROWS, HD), jnp.bfloat16),
            jax.ShapeDtypeStruct((3, 2, ROWS, HD), jnp.bfloat16),
        ]
        held = [pltpu.VMEM((TALL, 1152), jnp.float32)] + [pltpu.VMEM((ROWS, HD), jnp.float32)] * 2
        scratch = held + scratch
    else:
        out_shape = [acc, wide, wide] if state else [acc, wide, wide, wide]
    if mods is None:
        out_shape.append(jax.ShapeDtypeStruct((n, MODROWS, 640), jnp.bfloat16))
    out = pl.pallas_call(
        functools.partial(kernel, which, mods is not None),
        in_specs=[VMEM] * len(args),
        out_specs=[VMEM] * len(out_shape),
        out_shape=out_shape,
        scratch_shapes=scratch,
        compiler_params=pltpu.CompilerParams(vmem_limit_bytes=12 * 2**20),
        cost_estimate=cost(2 * TALL * n * 640 * 1152, n * 640 * 1152 * 2 + 3 * 2**20),
        name="qkv_part",
    )(*args)
    return (out[:-1], out[-1]) if mods is None else (out, mods)


LOG2E = 1.4426950408889634
SCORE = HD ** (-0.5) * LOG2E


def own_frame(q_ref, kv_ref, top_ref, sum_ref, acc_ref):
    for i in range(3):
        scores = nt_dot(q_ref[i], kv_ref[i, 0]) * SCORE
        top = jnp.max(scores, axis=-1, keepdims=True)
        weights = jnp.exp2(scores - top)
        top_ref[i] = jnp.broadcast_to(top, (ROWS, HD))
        sum_ref[i] = jnp.broadcast_to(jnp.sum(weights, axis=-1, keepdims=True), (ROWS, HD))
        acc_ref[i] = jnp.dot(
            weights.astype(jnp.bfloat16), kv_ref[i, 1], preferred_element_type=jnp.float32
        )


def run_own_frame(q, kv):
    wide = jax.ShapeDtypeStruct((3, ROWS, HD), jnp.float32)
    return pl.pallas_call(
        own_frame,
        in_specs=[VMEM] * 2,
        out_specs=[VMEM] * 3,
        out_shape=[wide] * 3,
        compiler_params=pltpu.CompilerParams(vmem_limit_bytes=12 * 2**20),
        cost_estimate=cost(4 * ROWS * ROWS * 384, 2 * 2**20),
        name="own_frame",
    )(q, kv)


def neighbours(
    reach_ref, q_ref, top_ref, sum_ref, acc_ref, near_kv, far_kv, out_ref
):
    position = lax.axis_index("queue")
    row = lax.broadcasted_iota(jnp.int32, (ROWS, ROWS), 0)
    col = lax.broadcasted_iota(jnp.int32, (ROWS, ROWS), 1)
    reach = reach_ref[...]
    distance = jnp.abs(col - row)
    near_seen = distance < reach
    far_seen = distance < jnp.where((position > 0) & (position < NQ - 1), reach, 0)
    for i in range(3):
        q = q_ref[i]
        near = jnp.where(near_seen, nt_dot(q, near_kv[i, 0]) * SCORE, -1e30)
        far = jnp.where(far_seen, nt_dot(q, far_kv[i, 0]) * SCORE, -1e30)
        own_top = top_ref[i][:, :1]
        top = jnp.maximum(own_top, jnp.max(jnp.maximum(near, far), axis=-1, keepdims=True))
        own_scale = jnp.exp2(own_top - top)
        near = jnp.exp2(near - top)
        far = jnp.exp2(far - top)
        total = sum_ref[i][:, :1] * own_scale + jnp.sum(near + far, axis=-1, keepdims=True)
        acc = acc_ref[i] * own_scale
        acc = acc + jnp.dot(
            near.astype(jnp.bfloat16), near_kv[i, 1], preferred_element_type=jnp.float32
        )
        acc = acc + jnp.dot(
            far.astype(jnp.bfloat16), far_kv[i, 1], preferred_element_type=jnp.float32
        )
        out_ref[:, i * HD : (i + 1) * HD] = (acc / total).astype(jnp.bfloat16)


def run_neighbours(reach, q, own, near, far):
    return pl.pallas_call(
        neighbours,
        in_specs=[VMEM] * 7,
        out_specs=VMEM,
        out_shape=jax.ShapeDtypeStruct((ROWS, 3 * HD), jnp.bfloat16),
        compiler_params=pltpu.CompilerParams(vmem_limit_bytes=12 * 2**20),
        cost_estimate=cost(8 * ROWS * ROWS * 384, 3 * 2**20),
        name="neighbours",
    )(reach, q, *own, near, far)


def place(w_ref, out_ref):
    h = lax.axis_index("queue") // 16
    for a in range(NT):
        half = lax.rem(a // 4 + h, 2)
        for j in range(4):
            out_ref[a, j * 160 : (j + 1) * 160, :] = w_ref[a % 4, j, half]


def run_place(w_whole):
    return pl.pallas_call(
        place,
        in_specs=[VMEM],
        out_specs=VMEM,
        out_shape=jax.ShapeDtypeStruct((NT, 640, 384), jnp.bfloat16),
        compiler_params=pltpu.CompilerParams(vmem_limit_bytes=8 * 2**20),
        cost_estimate=cost(0, 8 * 2**20),
        name="place",
    )(w_whole)


def add_projected(which, blocks, w_ref, total):
    ids = source_ids()
    for at, block in zip(which, blocks):
        part = nt_dot(block[...], w_ref[ids[at]])
        total = part if total is None else total + part
    return total


def project_part(which, *refs):
    n = len(which)
    blocks, w_ref, more = refs[:n], refs[n], refs[n + 1 : -1]
    refs[-1][...] = add_projected(which, blocks, w_ref, more[0][...] if more else None)


def run_project_part(which, blocks, w_whole, total=None):
    more = [] if total is None else [total]
    return pl.pallas_call(
        functools.partial(project_part, which),
        in_specs=[VMEM] * (len(which) + 1 + len(more)),
        out_specs=VMEM,
        out_shape=jax.ShapeDtypeStruct((ROWS, 640), jnp.float32),
        compiler_params=pltpu.CompilerParams(vmem_limit_bytes=12 * 2**20),
        cost_estimate=cost(2 * ROWS * 384 * 640 * len(which), 3 * 2**20),
        name="project_part",
    )(*blocks, w_whole, *more)


def stepped(which, level_ref, table_ref, *refs):
    n = len(which)
    w_ref, total_ref, x_ref, mods_ref = refs[n : n + 4]
    total = add_projected(which, refs[:n], w_ref, total_ref[...])
    level = level_ref[0]
    fall = (table_ref[level + 1] - table_ref[level]).astype(jnp.float32)
    step_size = jnp.full((1, 640), fall, jnp.float32) / 1000.0
    x = x_ref[...].astype(jnp.float32)
    result = x + mods_ref[0][2:3].astype(jnp.float32) * total
    return result, (x + step_size * result).astype(jnp.bfloat16)


def project_middle(which, *refs):
    fresh_ref, out_ref = refs[-2:]
    _, moved = stepped(which, *refs[:-2])
    out_ref[...] = jnp.where(lax.axis_index("queue") == NQ - 1, fresh_ref[...], moved)


def project_last(which, *refs):
    out_ref, velocity_ref = refs[-2:]
    result, moved = stepped(which, *refs[:-2])
    out_ref[...] = moved
    velocity_ref[...] = result.astype(jnp.bfloat16)


def run_project(which, times, blocks, w_whole, total, x, mods, fresh=None):
    block = jax.ShapeDtypeStruct((ROWS, 640), jnp.bfloat16)
    more = [] if fresh is None else [fresh]
    args = [*blocks, w_whole, total, x, mods, *more]
    return pl.pallas_call(
        functools.partial(project_middle if more else project_last, which),
        in_specs=[SMEM] * 2 + [VMEM] * len(args),
        out_specs=VMEM if more else [VMEM, VMEM],
        out_shape=block if more else [block, block],
        compiler_params=pltpu.CompilerParams(vmem_limit_bytes=12 * 2**20),
        cost_estimate=cost(2 * ROWS * 384 * 640 * len(which), 3 * 2**20),
        name="project",
    )(*times, *args)


def body(
    latents,
    fresh_noise,
    frame_level,
    timestep_table,
    modulation,
    w_query,
    w_key,
    w_value,
    qk_gain,
    w_out,
    reach,
):
    mod_rows = lax.dynamic_index_in_dim(modulation, frame_level[0], 0, keepdims=False)
    times = (frame_level, timestep_table)
    reach_rows = reach[:, None]
    weights = (w_query, w_key, w_value)
    inner = along_queue(lambda h, z, c: q_of(h, z, c + 1))
    outer = [(i, i + 1 if i % 2 else i - 1) for i in range(1, NQ - 1)]

    def halo(kv):
        return lax.ppermute(kv, "queue", outer), lax.ppermute(kv, "queue", inner)

    def qkv(mods):
        def start(block):
            state, kept = run_part(
                first_part, (0,), [block], mods and mods[0], weights, ()
            )
            return state, [kept]

        def more(which, n):
            def run(blocks, begun):
                (*state, center), kept = begun
                state, other = run_part(
                    middle_part, which, blocks, mods and mods[n], weights, [*state, center]
                )
                return [*state, center], [*kept, other]

            return run

        return start, more((1, 2, 3), 1), more((4, 5, 6), 2)

    def qkv_last(block, going, mods):
        state, kept = going
        (q_heads, kv), other = run_part(
            last_part, (7,), [block], mods and mods[3], weights, state, qk_gain
        )
        return q_heads, kv, [*kept, other]

    payload = jnp.concatenate(
        [latents, mod_rows, jnp.zeros((MODROWS - 3, latents.shape[1]), latents.dtype)], axis=0
    )
    turned = transposed(w_out.T)
    pair = jnp.concatenate([turned, lax.ppermute(turned, "queue", FAR)], axis=0)
    w_whole = lax.all_gather(pair, "queue", axis_index_groups=RING).reshape(4, 4, 2, 160, 384)
    weights = after(weights, pair)
    last, going = gather_blocks(payload, *qkv(None))
    q_heads, kv, mods = qkv_last(last, going, None)
    far, near = halo(kv)
    own = run_own_frame(q_heads, kv)
    attended = run_neighbours(reach_rows, q_heads, own, near, far)
    w_whole = run_place(w_whole)

    def project_start(block):
        return block

    def project_early(blocks, begun):
        return run_project_part((0, 1, 2, 3), [begun, *blocks], w_whole)

    def project_late(blocks, begun):
        return run_project_part((4, 5, 6), blocks, w_whole, begun)

    def finish(attended, frame, hold, *fresh):
        last, total = gather_blocks(attended, project_start, project_early, project_late, hold)
        return run_project((7,), times, [last], w_whole, total, frame, mods[0], *fresh)

    leaving = finish(attended, latents, False, fresh_noise)
    advanced = next_frame(leaving)
    last, going = gather_blocks(advanced, *qkv(mods))
    q_heads, kv, _ = qkv_last(last, going, mods)
    far, near = halo(kv)
    own = run_own_frame(q_heads, kv)
    attended = run_neighbours(reach_rows, q_heads, own, near, far)
    return tuple(finish(attended, advanced, True))


def solution(mesh):
    placed = (
        P("queue", "tensor"),
        P(None, "tensor"),
        P("queue"),
        P(),
        P(None, None, "tensor"),
        P(None, "tensor"),
        P(None, "tensor"),
        P(None, "tensor"),
        P(None, "tensor"),
        P("tensor", "queue"),
        P("queue"),
    )
    return jax.shard_map(
        body,
        mesh=mesh,
        in_specs=placed,
        out_specs=(P("queue", "tensor"), P("queue", "tensor")),
        check_vma=False,
    )
```

```python
import functools

import jax
import jax.numpy as jnp
from jax import lax
from jax.experimental import pallas as pl
from jax.experimental.pallas import tpu as pltpu
from jax.sharding import PartitionSpec as P

D = 5120
HD = 128
ROWS = 256
NQ = 32
NT = 8
MODROWS = 16
BOTH = ("queue", "tensor")


def t_of(y, x):
    return (y % 4) * 2 + x % 2


def q_of(h, z, c):
    return ((h % 2) * 8 + z % 8) * 2 + c % 2


def along_tensor(move):
    return [(t_of(y, x), move(y, x)) for y in range(4) for x in range(2)]


def along_queue(move):
    return [(q_of(h, z, c), move(h, z, c)) for h in range(2) for z in range(8) for c in range(2)]


def other_near(y):
    return (y + 1) % 4 if y % 2 else (y - 1) % 4


SIDE = along_tensor(lambda y, x: t_of(y, x + 1))
NEAR = along_tensor(lambda y, x: t_of(y ^ 1, x))
BACK = along_tensor(lambda y, x: t_of(other_near(y), x))
FAR = along_queue(lambda h, z, c: q_of(h + 1, z, c))
RING = [[q_of(h, z, c) for z in range(8) for c in range(2)] for h in range(2)]


def hold_all(values):
    return lax.optimization_barrier(values)


def gather_blocks(block, start, early, late, hold=True):
    near = lax.ppermute(block, "tensor", NEAR)
    back = lax.ppermute(block, "tensor", BACK)
    side = lax.ppermute(block, "tensor", SIDE)
    begun = start(block, (side, near, back))
    if hold:
        back, near, side, begun = hold_all((back, near, side, begun))
    far = lax.ppermute(back, "tensor", NEAR)
    side_back = lax.ppermute(side, "tensor", BACK)
    side_near = lax.ppermute(near, "tensor", SIDE)
    begun = early([side, near, back], begun)
    if hold:
        far, begun = hold_all((far, begun))
    side_far = lax.ppermute(far, "tensor", SIDE)
    going = late([far, side_near, side_back], begun)
    return side_far, going


def after(value, *others):
    return lax.optimization_barrier((value, *others))[0]


def source_ids():
    t = lax.axis_index("tensor")
    y, x = t // 2, t % 2
    near, back, far = y ^ 1, (y + 2 * (y % 2) - 1) % 4, y ^ 2
    pairs = [(y, x), (y, 1 - x), (near, x), (back, x), (far, x), (near, 1 - x), (back, 1 - x), (far, 1 - x)]
    return [2 * a + b for a, b in pairs]


def transposed(block):
    route = [
        ((4 * t + j) * NT + a, (4 * a + j) * NT + t)
        for t in range(NT)
        for j in range(4)
        for a in range(NT)
    ]
    return lax.ppermute(block, BOTH, route)


def next_frame(block):
    return lax.ppermute(block, "queue", [(i, (i + 1) % NQ) for i in range(NQ)])


def nt_dot(a, b):
    return lax.dot_general(a, b, (((1,), (1,)), ((), ())), preferred_element_type=jnp.float32)


VMEM = pl.BlockSpec(memory_space=pltpu.VMEM)
SMEM = pl.BlockSpec(memory_space=pltpu.SMEM)
CHUNK = 64
TALL = ROWS + MODROWS


def add_stats(blocks, total_ref, square_ref, fresh):
    def rows_at(r, carry):
        at = pl.ds(pl.multiple_of(r * CHUNK, CHUNK), CHUNK)
        if fresh:
            total = jnp.zeros((CHUNK, HD), jnp.float32)
            square = jnp.zeros((CHUNK, HD), jnp.float32)
        else:
            total, square = total_ref[at, :], square_ref[at, :]
        for block in blocks:
            for j in range(5):
                x = block[at, j * HD : (j + 1) * HD].astype(jnp.float32)
                total = total + x
                square = square + x * x
        total_ref[at, :] = total
        square_ref[at, :] = square
        return carry

    lax.fori_loop(0, ROWS // CHUNK, rows_at, 0)


def scaled_block(block, mods, center_ref, a_ref):
    line = lax.broadcasted_iota(jnp.int32, (MODROWS, HD), 0)
    for j in range(5):
        cols = slice(j * HD, (j + 1) * HD)
        rows = mods[:, cols].astype(jnp.float32)
        shift, scale = rows[0:1], 1.0 + rows[1:2]
        high = scale.astype(jnp.bfloat16).astype(jnp.float32)
        extra = jnp.where(
            line == 0,
            shift,
            jnp.where(line == 1, high, jnp.where(line == 2, scale - high, 0.0)),
        )
        a_ref[ROWS:TALL, cols] = extra.astype(jnp.bfloat16)
        for r in range(0, ROWS, CHUNK):
            x = block[r : r + CHUNK, cols].astype(jnp.float32)
            y = (x - center_ref[r : r + CHUNK, :]) * scale
            a_ref[r : r + CHUNK, cols] = y.astype(jnp.bfloat16)


def add_products(which, a_ref, weights, out_ref, total_in):
    ids = source_ids()
    for n, w_ref in enumerate(weights):
        cols = slice(n * 384, (n + 1) * 384)
        total = None if total_in is None else total_in[:, cols]
        for i, at in enumerate(which):
            rows = pl.ds(pl.multiple_of(ids[at] * 640, HD), 640)
            part = jnp.dot(a_ref[i], w_ref[rows, :], preferred_element_type=jnp.float32)
            total = part if total is None else total + part
        out_ref[:, cols] = total


def scaled_blocks(blocks, mods_ref, given, center_ref, a_ref):
    for i, block in enumerate(blocks):
        if not given:
            mods_ref[i] = block[ROWS:TALL, :]
        scaled_block(block, mods_ref.at[i], center_ref, a_ref.at[i])


def split_refs(n, given, refs, scratches=1):
    blocks, refs = refs[:n], refs[n:]
    if given:
        return blocks, refs[0], refs[1:]
    at = len(refs) - scratches - 1
    return blocks, refs[at], refs[:at] + refs[at + 1 :]


def first_part(which, given, *refs):
    n = len(which)
    blocks, mods_ref, refs = split_refs(n, given, refs)
    wq, wk, wv, acc_ref, total_ref, square_ref, center_ref, a_ref = refs
    add_stats(blocks, total_ref, square_ref, True)
    center = jnp.sum(total_ref[...], axis=1, keepdims=True) / (n * 640)
    center_ref[...] = jnp.broadcast_to(center, (ROWS, HD))
    scaled_blocks(blocks, mods_ref, given, center_ref, a_ref)
    add_products(which, a_ref, (wq, wk, wv), acc_ref, None)


def middle_part(which, given, *refs):
    blocks, mods_ref, refs = split_refs(len(which), given, refs)
    wq, wk, wv, acc_in, total_in, square_in, center_ref = refs[:7]
    acc_ref, total_ref, square_ref, a_ref = refs[7:]
    total_ref[...] = total_in[...]
    square_ref[...] = square_in[...]
    add_stats(blocks, total_ref, square_ref, False)
    scaled_blocks(blocks, mods_ref, given, center_ref, a_ref)
    add_products(which, a_ref, (wq, wk, wv), acc_ref, acc_in)


def head_norm(proj, gain):
    scale = lax.rsqrt(jnp.mean(proj * proj, axis=-1, keepdims=True) + 1e-06)
    return (proj * scale * gain).astype(jnp.bfloat16)


def last_part(which, given, *refs):
    blocks, mods_ref, refs = split_refs(len(which), given, refs, 4)
    wq, wk, wv, acc_in, total_in, square_in, center_ref, gain_ref = refs[:8]
    q_ref, kv_ref = refs[8:10]
    acc_ref, total_ref, square_ref, a_ref = refs[10:]
    total_ref[...] = total_in[...]
    square_ref[...] = square_in[...]
    add_stats(blocks, total_ref, square_ref, False)
    scaled_blocks(blocks, mods_ref, given, center_ref, a_ref)
    add_products(which, a_ref, (wq, wk, wv), acc_ref, acc_in)
    mean = jnp.sum(total_ref[...], axis=1, keepdims=True) / D
    var = jnp.sum(square_ref[...], axis=1, keepdims=True) / D - mean * mean
    inverse = lax.rsqrt(var + 1e-06)
    offset = (center_ref[:, :1] - mean) * inverse
    for n in range(9):
        cols = slice(n * HD, (n + 1) * HD)
        extra = acc_ref[ROWS:TALL, cols]
        proj = acc_ref[:ROWS, cols] * inverse + offset * (extra[1:2] + extra[2:3]) + extra[0:1]
        if n < 3:
            q_ref[n] = head_norm(proj, gain_ref[n // 3 : n // 3 + 1, n % 3 * HD : (n % 3 + 1) * HD])
        elif n < 6:
            kv_ref[n - 3, 0] = head_norm(proj, gain_ref[n // 3 : n // 3 + 1, n % 3 * HD : (n % 3 + 1) * HD])
        else:
            kv_ref[n - 6, 1] = proj.astype(jnp.bfloat16)


def cost(flops, nbytes):
    return pl.CostEstimate(flops=flops, bytes_accessed=nbytes, transcendentals=0)


def run_part(kernel, which, blocks, mods, weights, state, gain=None):
    n = len(which)
    wide = jax.ShapeDtypeStruct((ROWS, HD), jnp.float32)
    acc = jax.ShapeDtypeStruct((TALL, 1152), jnp.float32)
    args = [*blocks] + ([] if mods is None else [mods])
    args += [*weights, *state] + ([] if gain is None else [gain])
    scratch = [
        pltpu.VMEM((n, TALL, 640), jnp.bfloat16),
    ]
    if gain is not None:
        out_shape = [
            jax.ShapeDtypeStruct((3, ROWS, HD), jnp.bfloat16),
            jax.ShapeDtypeStruct((3, 2, ROWS, HD), jnp.bfloat16),
        ]
        held = [pltpu.VMEM((TALL, 1152), jnp.float32)] + [pltpu.VMEM((ROWS, HD), jnp.float32)] * 2
        scratch = held + scratch
    else:
        out_shape = [acc, wide, wide] if state else [acc, wide, wide, wide]
    if mods is None:
        out_shape.append(jax.ShapeDtypeStruct((n, MODROWS, 640), jnp.bfloat16))
    out = pl.pallas_call(
        functools.partial(kernel, which, mods is not None),
        in_specs=[VMEM] * len(args),
        out_specs=[VMEM] * len(out_shape),
        out_shape=out_shape,
        scratch_shapes=scratch,
        compiler_params=pltpu.CompilerParams(vmem_limit_bytes=12 * 2**20),
        cost_estimate=cost(2 * TALL * n * 640 * 1152, n * 640 * 1152 * 2 + 3 * 2**20),
        name="qkv_part",
    )(*args)
    return (out[:-1], out[-1]) if mods is None else (out, mods)


LOG2E = 1.4426950408889634
SCORE = HD ** (-0.5) * LOG2E


def own_frame(q_ref, kv_ref, top_ref, sum_ref, acc_ref):
    for i in range(3):
        scores = nt_dot(q_ref[i], kv_ref[i, 0]) * SCORE
        top = jnp.max(scores, axis=-1, keepdims=True)
        weights = jnp.exp2(scores - top)
        top_ref[i] = jnp.broadcast_to(top, (ROWS, HD))
        sum_ref[i] = jnp.broadcast_to(jnp.sum(weights, axis=-1, keepdims=True), (ROWS, HD))
        acc_ref[i] = jnp.dot(
            weights.astype(jnp.bfloat16), kv_ref[i, 1], preferred_element_type=jnp.float32
        )


def run_own_frame(q, kv):
    wide = jax.ShapeDtypeStruct((3, ROWS, HD), jnp.float32)
    return pl.pallas_call(
        own_frame,
        in_specs=[VMEM] * 2,
        out_specs=[VMEM] * 3,
        out_shape=[wide] * 3,
        compiler_params=pltpu.CompilerParams(vmem_limit_bytes=12 * 2**20),
        cost_estimate=cost(4 * ROWS * ROWS * 384, 2 * 2**20),
        name="own_frame",
    )(q, kv)


def neighbours(
    reach_ref, q_ref, top_ref, sum_ref, acc_ref, near_kv, far_kv, out_ref
):
    position = lax.axis_index("queue")
    row = lax.broadcasted_iota(jnp.int32, (ROWS, ROWS), 0)
    col = lax.broadcasted_iota(jnp.int32, (ROWS, ROWS), 1)
    reach = reach_ref[...]
    distance = jnp.abs(col - row)
    near_seen = distance < reach
    far_seen = distance < jnp.where((position > 0) & (position < NQ - 1), reach, 0)
    for i in range(3):
        q = q_ref[i]
        near = jnp.where(near_seen, nt_dot(q, near_kv[i, 0]) * SCORE, -1e30)
        far = jnp.where(far_seen, nt_dot(q, far_kv[i, 0]) * SCORE, -1e30)
        own_top = top_ref[i][:, :1]
        top = jnp.maximum(own_top, jnp.max(jnp.maximum(near, far), axis=-1, keepdims=True))
        own_scale = jnp.exp2(own_top - top)
        near = jnp.exp2(near - top)
        far = jnp.exp2(far - top)
        total = sum_ref[i][:, :1] * own_scale + jnp.sum(near + far, axis=-1, keepdims=True)
        acc = acc_ref[i] * own_scale
        acc = acc + jnp.dot(
            near.astype(jnp.bfloat16), near_kv[i, 1], preferred_element_type=jnp.float32
        )
        acc = acc + jnp.dot(
            far.astype(jnp.bfloat16), far_kv[i, 1], preferred_element_type=jnp.float32
        )
        out_ref[:, i * HD : (i + 1) * HD] = (acc / total).astype(jnp.bfloat16)


def run_neighbours(reach, q, own, near, far):
    return pl.pallas_call(
        neighbours,
        in_specs=[VMEM] * 7,
        out_specs=VMEM,
        out_shape=jax.ShapeDtypeStruct((ROWS, 3 * HD), jnp.bfloat16),
        compiler_params=pltpu.CompilerParams(vmem_limit_bytes=12 * 2**20),
        cost_estimate=cost(8 * ROWS * ROWS * 384, 3 * 2**20),
        name="neighbours",
    )(reach, q, *own, near, far)


def place(w_ref, out_ref):
    h = lax.axis_index("queue") // 16
    for a in range(NT):
        half = lax.rem(a // 4 + h, 2)
        for j in range(4):
            out_ref[a, j * 160 : (j + 1) * 160, :] = w_ref[a % 4, j, half]


def run_place(w_whole):
    return pl.pallas_call(
        place,
        in_specs=[VMEM],
        out_specs=VMEM,
        out_shape=jax.ShapeDtypeStruct((NT, 640, 384), jnp.bfloat16),
        compiler_params=pltpu.CompilerParams(vmem_limit_bytes=8 * 2**20),
        cost_estimate=cost(0, 8 * 2**20),
        name="place",
    )(w_whole)


def add_projected(which, blocks, w_ref, total):
    ids = source_ids()
    for at, block in zip(which, blocks):
        part = nt_dot(block[...], w_ref[ids[at]])
        total = part if total is None else total + part
    return total


def project_part(which, *refs):
    n = len(which)
    blocks, w_ref, more = refs[:n], refs[n], refs[n + 1 : -1]
    refs[-1][...] = add_projected(which, blocks, w_ref, more[0][...] if more else None)


def run_project_part(which, blocks, w_whole, total=None):
    more = [] if total is None else [total]
    return pl.pallas_call(
        functools.partial(project_part, which),
        in_specs=[VMEM] * (len(which) + 1 + len(more)),
        out_specs=VMEM,
        out_shape=jax.ShapeDtypeStruct((ROWS, 640), jnp.float32),
        compiler_params=pltpu.CompilerParams(vmem_limit_bytes=12 * 2**20),
        cost_estimate=cost(2 * ROWS * 384 * 640 * len(which), 3 * 2**20),
        name="project_part",
    )(*blocks, w_whole, *more)


def stepped(which, level_ref, table_ref, *refs):
    n = len(which)
    w_ref, total_ref, x_ref, mods_ref = refs[n : n + 4]
    total = add_projected(which, refs[:n], w_ref, total_ref[...])
    level = level_ref[0]
    fall = (table_ref[level + 1] - table_ref[level]).astype(jnp.float32)
    step_size = jnp.full((1, 640), fall, jnp.float32) / 1000.0
    x = x_ref[...].astype(jnp.float32)
    result = x + mods_ref[0][2:3].astype(jnp.float32) * total
    return result, (x + step_size * result).astype(jnp.bfloat16)


def project_middle(which, *refs):
    fresh_ref, out_ref = refs[-2:]
    _, moved = stepped(which, *refs[:-2])
    out_ref[...] = jnp.where(lax.axis_index("queue") == NQ - 1, fresh_ref[...], moved)


def project_last(which, *refs):
    out_ref, velocity_ref = refs[-2:]
    result, moved = stepped(which, *refs[:-2])
    out_ref[...] = moved
    velocity_ref[...] = result.astype(jnp.bfloat16)


def run_project(which, times, blocks, w_whole, total, x, mods, fresh=None):
    block = jax.ShapeDtypeStruct((ROWS, 640), jnp.bfloat16)
    more = [] if fresh is None else [fresh]
    args = [*blocks, w_whole, total, x, mods, *more]
    return pl.pallas_call(
        functools.partial(project_middle if more else project_last, which),
        in_specs=[SMEM] * 2 + [VMEM] * len(args),
        out_specs=VMEM if more else [VMEM, VMEM],
        out_shape=block if more else [block, block],
        compiler_params=pltpu.CompilerParams(vmem_limit_bytes=12 * 2**20),
        cost_estimate=cost(2 * ROWS * 384 * 640 * len(which), 3 * 2**20),
        name="project",
    )(*times, *args)


def body(
    latents,
    fresh_noise,
    frame_level,
    timestep_table,
    modulation,
    w_query,
    w_key,
    w_value,
    qk_gain,
    w_out,
    reach,
):
    mod_rows = lax.dynamic_index_in_dim(modulation, frame_level[0], 0, keepdims=False)
    times = (frame_level, timestep_table)
    reach_rows = reach[:, None]
    weights = (w_query, w_key, w_value)
    inner = along_queue(lambda h, z, c: q_of(h, z, c + 1))
    outer = [(i, i + 1 if i % 2 else i - 1) for i in range(1, NQ - 1)]

    def halo(kv):
        return lax.ppermute(kv, "queue", outer), lax.ppermute(kv, "queue", inner)

    def qkv(mods, weights):
        def start(block, firsts):
            state, kept = run_part(
                first_part, (0,), [block], mods and mods[0], weights, ()
            )
            return state, [kept]

        def more(which, n):
            def run(blocks, begun):
                (*state, center), kept = begun
                state, other = run_part(
                    middle_part, which, blocks, mods and mods[n], weights, [*state, center]
                )
                return [*state, center], [*kept, other]

            return run

        return start, more((1, 2, 3), 1), more((4, 5, 6), 2)

    def qkv_last(block, going, mods, weights):
        state, kept = going
        (q_heads, kv), other = run_part(
            last_part, (7,), [block], mods and mods[3], weights, state, qk_gain
        )
        return q_heads, kv, [*kept, other]

    payload = jnp.concatenate(
        [latents, mod_rows, jnp.zeros((MODROWS - 3, latents.shape[1]), latents.dtype)], axis=0
    )
    turned = transposed(w_out.T)

    parts = []

    def gather_w_out(block, firsts):
        crossed = lax.ppermute(turned, "queue", FAR)
        pair = jnp.concatenate([turned, crossed], axis=0)
        w_all = lax.all_gather(pair, "queue", axis_index_groups=RING)
        parts.append(w_all.reshape(4, 4, 2, 160, 384))
        return pair

    def early(blocks, begun):
        held = after(weights, begun)
        first, middle, _ = qkv(None, held)
        return middle(blocks, first(payload, None)), held

    def late(blocks, begun):
        state, held = begun
        return held, qkv(None, held)[2](blocks, state)

    payload = after(payload, turned)
    last, (weights, going) = gather_blocks(payload, gather_w_out, early, late)
    q_heads, kv, mods = qkv_last(last, going, None, weights)
    far, near = halo(kv)
    own = run_own_frame(q_heads, kv)
    w_whole = run_place(after(parts[0], own[0]))
    attended = run_neighbours(reach_rows, after(q_heads, w_whole), own, near, far)

    def project_start(block, firsts):
        return block

    def project_early(blocks, begun):
        return run_project_part((0, 1, 2, 3), [begun, *blocks], w_whole)

    def project_late(blocks, begun):
        return run_project_part((4, 5, 6), blocks, w_whole, begun)

    def finish(attended, frame, hold, *fresh):
        last, total = gather_blocks(attended, project_start, project_early, project_late, hold)
        return run_project((7,), times, [last], w_whole, total, frame, mods[0], *fresh)

    leaving = finish(attended, latents, False, fresh_noise)
    advanced = next_frame(leaving)
    last, going = gather_blocks(advanced, *qkv(mods, weights))
    q_heads, kv, _ = qkv_last(last, going, mods, weights)
    far, near = halo(kv)
    own = run_own_frame(q_heads, kv)
    attended = run_neighbours(reach_rows, q_heads, own, near, far)
    return tuple(finish(attended, advanced, False))


def solution(mesh):
    placed = (
        P("queue", "tensor"),
        P(None, "tensor"),
        P("queue"),
        P(),
        P(None, None, "tensor"),
        P(None, "tensor"),
        P(None, "tensor"),
        P(None, "tensor"),
        P(None, "tensor"),
        P("tensor", "queue"),
        P("queue"),
    )
    return jax.shard_map(
        body,
        mesh=mesh,
        in_specs=placed,
        out_specs=(P("queue", "tensor"), P("queue", "tensor")),
        check_vma=False,
    )
```

```python
import functools

import jax
import jax.numpy as jnp
from jax import lax
from jax.experimental import pallas as pl
from jax.experimental.pallas import tpu as pltpu
from jax.sharding import PartitionSpec as P

D = 5120
HD = 128
ROWS = 256
NQ = 32
NT = 8
MODROWS = 16
BOTH = ("queue", "tensor")


def t_of(y, x):
    return (y % 4) * 2 + x % 2


def q_of(h, z, c):
    return ((h % 2) * 8 + z % 8) * 2 + c % 2


def along_tensor(move):
    return [(t_of(y, x), move(y, x)) for y in range(4) for x in range(2)]


def along_queue(move):
    return [(q_of(h, z, c), move(h, z, c)) for h in range(2) for z in range(8) for c in range(2)]


def other_near(y):
    return (y + 1) % 4 if y % 2 else (y - 1) % 4


SIDE = along_tensor(lambda y, x: t_of(y, x + 1))
NEAR = along_tensor(lambda y, x: t_of(y ^ 1, x))
BACK = along_tensor(lambda y, x: t_of(other_near(y), x))
FAR = along_queue(lambda h, z, c: q_of(h + 1, z, c))
RING = [[q_of(h, z, c) for z in range(8) for c in range(2)] for h in range(2)]


def hold_all(values):
    return lax.optimization_barrier(values)


def gather_blocks(block, start, early, late, hold=True):
    near = lax.ppermute(block, "tensor", NEAR)
    back = lax.ppermute(block, "tensor", BACK)
    side = lax.ppermute(block, "tensor", SIDE)
    begun = start(block, (side, near, back))
    if hold:
        back, near, side, begun = hold_all((back, near, side, begun))
    far = lax.ppermute(back, "tensor", NEAR)
    side_back = lax.ppermute(side, "tensor", BACK)
    side_near = lax.ppermute(near, "tensor", SIDE)
    begun = early([side, near, back], begun)
    if hold:
        far, begun = hold_all((far, begun))
    side_far = lax.ppermute(far, "tensor", SIDE)
    going = late([far, side_near, side_back], begun)
    return side_far, going


def after(value, *others):
    return lax.optimization_barrier((value, *others))[0]


def source_ids():
    t = lax.axis_index("tensor")
    y, x = t // 2, t % 2
    near, back, far = y ^ 1, (y + 2 * (y % 2) - 1) % 4, y ^ 2
    pairs = [(y, x), (y, 1 - x), (near, x), (back, x), (far, x), (near, 1 - x), (back, 1 - x), (far, 1 - x)]
    return [2 * a + b for a, b in pairs]


def transposed(block):
    route = [
        ((4 * t + j) * NT + a, (4 * a + j) * NT + t)
        for t in range(NT)
        for j in range(4)
        for a in range(NT)
    ]
    return lax.ppermute(block, BOTH, route)


def next_frame(block):
    return lax.ppermute(block, "queue", [(i, (i + 1) % NQ) for i in range(NQ)])


def nt_dot(a, b):
    return lax.dot_general(a, b, (((1,), (1,)), ((), ())), preferred_element_type=jnp.float32)


VMEM = pl.BlockSpec(memory_space=pltpu.VMEM)
SMEM = pl.BlockSpec(memory_space=pltpu.SMEM)
CHUNK = 64
TALL = ROWS + MODROWS


def add_stats(blocks, total_ref, square_ref, fresh):
    def rows_at(r, carry):
        at = pl.ds(pl.multiple_of(r * CHUNK, CHUNK), CHUNK)
        if fresh:
            total = jnp.zeros((CHUNK, HD), jnp.float32)
            square = jnp.zeros((CHUNK, HD), jnp.float32)
        else:
            total, square = total_ref[at, :], square_ref[at, :]
        for block in blocks:
            for j in range(5):
                x = block[at, j * HD : (j + 1) * HD].astype(jnp.float32)
                total = total + x
                square = square + x * x
        total_ref[at, :] = total
        square_ref[at, :] = square
        return carry

    lax.fori_loop(0, ROWS // CHUNK, rows_at, 0)


def scaled_block(block, mods, center_ref, a_ref):
    line = lax.broadcasted_iota(jnp.int32, (MODROWS, HD), 0)
    for j in range(5):
        cols = slice(j * HD, (j + 1) * HD)
        rows = mods[:, cols].astype(jnp.float32)
        shift, scale = rows[0:1], 1.0 + rows[1:2]
        high = scale.astype(jnp.bfloat16).astype(jnp.float32)
        extra = jnp.where(
            line == 0,
            shift,
            jnp.where(line == 1, high, jnp.where(line == 2, scale - high, 0.0)),
        )
        a_ref[ROWS:TALL, cols] = extra.astype(jnp.bfloat16)
        for r in range(0, ROWS, CHUNK):
            x = block[r : r + CHUNK, cols].astype(jnp.float32)
            y = (x - center_ref[r : r + CHUNK, :]) * scale
            a_ref[r : r + CHUNK, cols] = y.astype(jnp.bfloat16)


def add_products(which, a_ref, weights, out_ref, total_in):
    ids = source_ids()
    for n, w_ref in enumerate(weights):
        cols = slice(n * 384, (n + 1) * 384)
        total = None if total_in is None else total_in[:, cols]
        for i, at in enumerate(which):
            rows = pl.ds(pl.multiple_of(ids[at] * 640, HD), 640)
            part = jnp.dot(a_ref[i], w_ref[rows, :], preferred_element_type=jnp.float32)
            total = part if total is None else total + part
        out_ref[:, cols] = total


def scaled_blocks(blocks, mods_ref, given, center_ref, a_ref):
    for i, block in enumerate(blocks):
        if not given:
            mods_ref[i] = block[ROWS:TALL, :]
        scaled_block(block, mods_ref.at[i], center_ref, a_ref.at[i])


def split_refs(n, given, refs, scratches=1):
    blocks, refs = refs[:n], refs[n:]
    if given:
        return blocks, refs[0], refs[1:]
    at = len(refs) - scratches - 1
    return blocks, refs[at], refs[:at] + refs[at + 1 :]


def first_part(which, given, *refs):
    n = len(which)
    blocks, mods_ref, refs = split_refs(n, given, refs)
    wq, wk, wv, acc_ref, total_ref, square_ref, center_ref, a_ref = refs
    add_stats(blocks, total_ref, square_ref, True)
    center = jnp.sum(total_ref[...], axis=1, keepdims=True) / (n * 640)
    center_ref[...] = jnp.broadcast_to(center, (ROWS, HD))
    scaled_blocks(blocks, mods_ref, given, center_ref, a_ref)
    add_products(which, a_ref, (wq, wk, wv), acc_ref, None)


def middle_part(which, given, *refs):
    blocks, mods_ref, refs = split_refs(len(which), given, refs)
    wq, wk, wv, acc_in, total_in, square_in, center_ref = refs[:7]
    acc_ref, total_ref, square_ref, a_ref = refs[7:]
    total_ref[...] = total_in[...]
    square_ref[...] = square_in[...]
    add_stats(blocks, total_ref, square_ref, False)
    scaled_blocks(blocks, mods_ref, given, center_ref, a_ref)
    add_products(which, a_ref, (wq, wk, wv), acc_ref, acc_in)


def head_norm(proj, gain):
    scale = lax.rsqrt(jnp.mean(proj * proj, axis=-1, keepdims=True) + 1e-06)
    return (proj * scale * gain).astype(jnp.bfloat16)


def last_part(which, given, *refs):
    blocks, mods_ref, refs = split_refs(len(which), given, refs, 4)
    wq, wk, wv, acc_in, total_in, square_in, center_ref, gain_ref = refs[:8]
    q_ref, kv_ref = refs[8:10]
    acc_ref, total_ref, square_ref, a_ref = refs[10:]
    total_ref[...] = total_in[...]
    square_ref[...] = square_in[...]
    add_stats(blocks, total_ref, square_ref, False)
    scaled_blocks(blocks, mods_ref, given, center_ref, a_ref)
    add_products(which, a_ref, (wq, wk, wv), acc_ref, acc_in)
    mean = jnp.sum(total_ref[...], axis=1, keepdims=True) / D
    var = jnp.sum(square_ref[...], axis=1, keepdims=True) / D - mean * mean
    inverse = lax.rsqrt(var + 1e-06)
    offset = (center_ref[:, :1] - mean) * inverse
    for n in range(9):
        cols = slice(n * HD, (n + 1) * HD)
        extra = acc_ref[ROWS:TALL, cols]
        proj = acc_ref[:ROWS, cols] * inverse + offset * (extra[1:2] + extra[2:3]) + extra[0:1]
        if n < 3:
            q_ref[n] = head_norm(proj, gain_ref[n // 3 : n // 3 + 1, n % 3 * HD : (n % 3 + 1) * HD])
        elif n < 6:
            kv_ref[n - 3, 0] = head_norm(proj, gain_ref[n // 3 : n // 3 + 1, n % 3 * HD : (n % 3 + 1) * HD])
        else:
            kv_ref[n - 6, 1] = proj.astype(jnp.bfloat16)


def cost(flops, nbytes):
    return pl.CostEstimate(flops=flops, bytes_accessed=nbytes, transcendentals=0)


def run_part(kernel, which, blocks, mods, weights, state, gain=None):
    n = len(which)
    wide = jax.ShapeDtypeStruct((ROWS, HD), jnp.float32)
    acc = jax.ShapeDtypeStruct((TALL, 1152), jnp.float32)
    args = [*blocks] + ([] if mods is None else [mods])
    args += [*weights, *state] + ([] if gain is None else [gain])
    scratch = [
        pltpu.VMEM((n, TALL, 640), jnp.bfloat16),
    ]
    if gain is not None:
        out_shape = [
            jax.ShapeDtypeStruct((3, ROWS, HD), jnp.bfloat16),
            jax.ShapeDtypeStruct((3, 2, ROWS, HD), jnp.bfloat16),
        ]
        held = [pltpu.VMEM((TALL, 1152), jnp.float32)] + [pltpu.VMEM((ROWS, HD), jnp.float32)] * 2
        scratch = held + scratch
    else:
        out_shape = [acc, wide, wide] if state else [acc, wide, wide, wide]
    if mods is None:
        out_shape.append(jax.ShapeDtypeStruct((n, MODROWS, 640), jnp.bfloat16))
    out = pl.pallas_call(
        functools.partial(kernel, which, mods is not None),
        in_specs=[VMEM] * len(args),
        out_specs=[VMEM] * len(out_shape),
        out_shape=out_shape,
        scratch_shapes=scratch,
        compiler_params=pltpu.CompilerParams(vmem_limit_bytes=12 * 2**20),
        cost_estimate=cost(2 * TALL * n * 640 * 1152, n * 640 * 1152 * 2 + 3 * 2**20),
        name="qkv_part",
    )(*args)
    return (out[:-1], out[-1]) if mods is None else (out, mods)


LOG2E = 1.4426950408889634
SCORE = HD ** (-0.5) * LOG2E


def own_frame(q_ref, kv_ref, top_ref, sum_ref, acc_ref):
    for i in range(3):
        scores = nt_dot(q_ref[i], kv_ref[i, 0]) * SCORE
        top = jnp.max(scores, axis=-1, keepdims=True)
        weights = jnp.exp2(scores - top)
        top_ref[i] = jnp.broadcast_to(top, (ROWS, HD))
        sum_ref[i] = jnp.broadcast_to(jnp.sum(weights, axis=-1, keepdims=True), (ROWS, HD))
        acc_ref[i] = jnp.dot(
            weights.astype(jnp.bfloat16), kv_ref[i, 1], preferred_element_type=jnp.float32
        )


def run_own_frame(q, kv):
    wide = jax.ShapeDtypeStruct((3, ROWS, HD), jnp.float32)
    return pl.pallas_call(
        own_frame,
        in_specs=[VMEM] * 2,
        out_specs=[VMEM] * 3,
        out_shape=[wide] * 3,
        compiler_params=pltpu.CompilerParams(vmem_limit_bytes=12 * 2**20),
        cost_estimate=cost(4 * ROWS * ROWS * 384, 2 * 2**20),
        name="own_frame",
    )(q, kv)


def neighbours(
    reach_ref, q_ref, top_ref, sum_ref, acc_ref, near_kv, far_kv, out_ref
):
    position = lax.axis_index("queue")
    row = lax.broadcasted_iota(jnp.int32, (ROWS, ROWS), 0)
    col = lax.broadcasted_iota(jnp.int32, (ROWS, ROWS), 1)
    reach = reach_ref[...]
    distance = jnp.abs(col - row)
    near_seen = distance < reach
    far_seen = distance < jnp.where((position > 0) & (position < NQ - 1), reach, 0)
    for i in range(3):
        q = q_ref[i]
        near = jnp.where(near_seen, nt_dot(q, near_kv[i, 0]) * SCORE, -1e30)
        far = jnp.where(far_seen, nt_dot(q, far_kv[i, 0]) * SCORE, -1e30)
        own_top = top_ref[i][:, :1]
        top = jnp.maximum(own_top, jnp.max(jnp.maximum(near, far), axis=-1, keepdims=True))
        own_scale = jnp.exp2(own_top - top)
        near = jnp.exp2(near - top)
        far = jnp.exp2(far - top)
        total = sum_ref[i][:, :1] * own_scale + jnp.sum(near + far, axis=-1, keepdims=True)
        acc = acc_ref[i] * own_scale
        acc = acc + jnp.dot(
            near.astype(jnp.bfloat16), near_kv[i, 1], preferred_element_type=jnp.float32
        )
        acc = acc + jnp.dot(
            far.astype(jnp.bfloat16), far_kv[i, 1], preferred_element_type=jnp.float32
        )
        out_ref[:, i * HD : (i + 1) * HD] = (acc / total).astype(jnp.bfloat16)


def run_neighbours(reach, q, own, near, far):
    return pl.pallas_call(
        neighbours,
        in_specs=[VMEM] * 7,
        out_specs=VMEM,
        out_shape=jax.ShapeDtypeStruct((ROWS, 3 * HD), jnp.bfloat16),
        compiler_params=pltpu.CompilerParams(vmem_limit_bytes=12 * 2**20),
        cost_estimate=cost(8 * ROWS * ROWS * 384, 3 * 2**20),
        name="neighbours",
    )(reach, q, *own, near, far)


def place(w_ref, out_ref):
    h = lax.axis_index("queue") // 16
    for a in range(NT):
        half = lax.rem(a // 4 + h, 2)
        for j in range(4):
            out_ref[a, j * 160 : (j + 1) * 160, :] = w_ref[a % 4, j, half]


def run_place(w_whole):
    return pl.pallas_call(
        place,
        in_specs=[VMEM],
        out_specs=VMEM,
        out_shape=jax.ShapeDtypeStruct((NT, 640, 384), jnp.bfloat16),
        compiler_params=pltpu.CompilerParams(vmem_limit_bytes=8 * 2**20),
        cost_estimate=cost(0, 8 * 2**20),
        name="place",
    )(w_whole)


def add_projected(which, blocks, w_ref, total):
    ids = source_ids()
    for at, block in zip(which, blocks):
        part = nt_dot(block[...], w_ref[ids[at]])
        total = part if total is None else total + part
    return total


def project_part(which, *refs):
    n = len(which)
    blocks, w_ref, more = refs[:n], refs[n], refs[n + 1 : -1]
    refs[-1][...] = add_projected(which, blocks, w_ref, more[0][...] if more else None)


def run_project_part(which, blocks, w_whole, total=None):
    more = [] if total is None else [total]
    return pl.pallas_call(
        functools.partial(project_part, which),
        in_specs=[VMEM] * (len(which) + 1 + len(more)),
        out_specs=VMEM,
        out_shape=jax.ShapeDtypeStruct((ROWS, 640), jnp.float32),
        compiler_params=pltpu.CompilerParams(vmem_limit_bytes=12 * 2**20),
        cost_estimate=cost(2 * ROWS * 384 * 640 * len(which), 3 * 2**20),
        name="project_part",
    )(*blocks, w_whole, *more)


def stepped(which, level_ref, table_ref, *refs):
    n = len(which)
    w_ref, total_ref, x_ref, mods_ref = refs[n : n + 4]
    total = add_projected(which, refs[:n], w_ref, total_ref[...])
    level = level_ref[0]
    fall = (table_ref[level + 1] - table_ref[level]).astype(jnp.float32)
    step_size = jnp.full((1, 640), fall, jnp.float32) / 1000.0
    x = x_ref[...].astype(jnp.float32)
    result = x + mods_ref[0][2:3].astype(jnp.float32) * total
    return result, (x + step_size * result).astype(jnp.bfloat16)


def project_middle(which, *refs):
    fresh_ref, out_ref = refs[-2:]
    _, moved = stepped(which, *refs[:-2])
    out_ref[...] = jnp.where(lax.axis_index("queue") == NQ - 1, fresh_ref[...], moved)


def project_last(which, *refs):
    out_ref, velocity_ref = refs[-2:]
    result, moved = stepped(which, *refs[:-2])
    out_ref[...] = moved
    velocity_ref[...] = result.astype(jnp.bfloat16)


def run_project(which, times, blocks, w_whole, total, x, mods, fresh=None):
    block = jax.ShapeDtypeStruct((ROWS, 640), jnp.bfloat16)
    more = [] if fresh is None else [fresh]
    args = [*blocks, w_whole, total, x, mods, *more]
    return pl.pallas_call(
        functools.partial(project_middle if more else project_last, which),
        in_specs=[SMEM] * 2 + [VMEM] * len(args),
        out_specs=VMEM if more else [VMEM, VMEM],
        out_shape=block if more else [block, block],
        compiler_params=pltpu.CompilerParams(vmem_limit_bytes=12 * 2**20),
        cost_estimate=cost(2 * ROWS * 384 * 640 * len(which), 3 * 2**20),
        name="project",
    )(*times, *args)


def body(
    latents,
    fresh_noise,
    frame_level,
    timestep_table,
    modulation,
    w_query,
    w_key,
    w_value,
    qk_gain,
    w_out,
    reach,
):
    mod_rows = lax.dynamic_index_in_dim(modulation, frame_level[0], 0, keepdims=False)
    times = (frame_level, timestep_table)
    reach_rows = reach[:, None]
    weights = (w_query, w_key, w_value)
    inner = along_queue(lambda h, z, c: q_of(h, z, c + 1))
    outer = [(i, i + 1 if i % 2 else i - 1) for i in range(1, NQ - 1)]

    def halo(kv):
        return lax.ppermute(kv, "queue", outer), lax.ppermute(kv, "queue", inner)

    def qkv(mods, weights):
        def start(block, firsts):
            state, kept = run_part(
                first_part, (0,), [block], mods and mods[0], weights, ()
            )
            return state, [kept]

        def more(which, n):
            def run(blocks, begun):
                (*state, center), kept = begun
                state, other = run_part(
                    middle_part, which, blocks, mods and mods[n], weights, [*state, center]
                )
                return [*state, center], [*kept, other]

            return run

        return start, more((1, 2, 3), 1), more((4, 5, 6), 2)

    def qkv_last(block, going, mods, weights):
        state, kept = going
        (q_heads, kv), other = run_part(
            last_part, (7,), [block], mods and mods[3], weights, state, qk_gain
        )
        return q_heads, kv, [*kept, other]

    payload = jnp.concatenate(
        [latents, mod_rows, jnp.zeros((MODROWS - 3, latents.shape[1]), latents.dtype)], axis=0
    )
    turned = transposed(w_out.T)

    parts = []

    def gather_w_out(block, firsts):
        crossed = lax.ppermute(turned, "queue", FAR)
        pair = jnp.concatenate([turned, crossed], axis=0)
        w_all = lax.all_gather(pair, "queue", axis_index_groups=RING)
        parts.append(w_all.reshape(4, 4, 2, 160, 384))
        held = after(weights, pair)
        return qkv(None, held)[0](block, firsts), held

    def early(blocks, begun):
        state, held = begun
        return qkv(None, held)[1](blocks, state), held

    def late(blocks, begun):
        state, held = begun
        return held, qkv(None, held)[2](blocks, state)

    payload = after(payload, turned)
    last, (weights, going) = gather_blocks(payload, gather_w_out, early, late)
    q_heads, kv, mods = qkv_last(last, going, None, weights)
    far, near = halo(kv)
    own = run_own_frame(q_heads, kv)
    attended = run_neighbours(reach_rows, q_heads, own, near, far)
    w_whole = run_place(after(parts[0], attended))

    def project_start(block, firsts):
        return block

    def project_early(blocks, begun):
        return run_project_part((0, 1, 2, 3), [begun, *blocks], w_whole)

    def project_late(blocks, begun):
        return run_project_part((4, 5, 6), blocks, w_whole, begun)

    def finish(attended, frame, hold, *fresh):
        last, total = gather_blocks(attended, project_start, project_early, project_late, hold)
        return run_project((7,), times, [last], w_whole, total, frame, mods[0], *fresh)

    leaving = finish(attended, latents, True, fresh_noise)
    advanced = next_frame(leaving)
    last, going = gather_blocks(advanced, *qkv(mods, weights))
    q_heads, kv, _ = qkv_last(last, going, mods, weights)
    far, near = halo(kv)
    own = run_own_frame(q_heads, kv)
    attended = run_neighbours(reach_rows, q_heads, own, near, far)
    return tuple(finish(attended, advanced, False))


def solution(mesh):
    placed = (
        P("queue", "tensor"),
        P(None, "tensor"),
        P("queue"),
        P(),
        P(None, None, "tensor"),
        P(None, "tensor"),
        P(None, "tensor"),
        P(None, "tensor"),
        P(None, "tensor"),
        P("tensor", "queue"),
        P("queue"),
    )
    return jax.shard_map(
        body,
        mesh=mesh,
        in_specs=placed,
        out_specs=(P("queue", "tensor"), P("queue", "tensor")),
        check_vma=False,
    )
```
